32 devices in a mesh: rows: 8 (over z, y), seq: 4 (over x, core).
Axes of the slice: x: 2, y: 2, z: 4, core: 2. Of those that a mesh axis runs over, the one named last changes fastest.
Arguments:
- tokens: bfloat16 [2, 8, 1024, 1152], P(None, 'rows', 'seq'), may hold values from -6 to 6
- lengths: int32 [2, 8, 4], P(None, 'rows'), may hold values from 1 to 1024, as said below
- norm1_gain: bfloat16 [1152], P(('rows', 'seq')), may hold values from 0.25 to 1.75
- norm1_bias: bfloat16 [1152], P(('rows', 'seq')), may hold values from -3 to 3
- w_query: bfloat16 [1152, 1152], P(('rows', 'seq')), may hold values from -0.1875 to 0.1875
- query_bias: bfloat16 [1152], P(('rows', 'seq')), may hold values from -3 to 3
- w_key: bfloat16 [1152, 1152], P(('rows', 'seq')), may hold values from -0.1875 to 0.1875
- w_value: bfloat16 [1152, 1152], P(('rows', 'seq')), may hold values from -0.1875 to 0.1875
- value_bias: bfloat16 [1152], P(('rows', 'seq')), may hold values from -3 to 3
- w_out: bfloat16 [1152, 1152], P(('rows', 'seq')), may hold values from -3 to 3
- out_bias: bfloat16 [1152], P(('rows', 'seq')), may hold values from -3 to 3
- norm2_gain: bfloat16 [1152], P(('rows', 'seq')), may hold values from 0.25 to 1.75
- norm2_bias: bfloat16 [1152], P(('rows', 'seq')), may hold values from -3 to 3
- w_up: bfloat16 [1152, 4304], P(('rows', 'seq')), may hold values from -0.1875 to 0.1875
- up_bias: bfloat16 [4304], replicated, may hold values from -3 to 3
- w_down: bfloat16 [4304, 1152], P(None, ('rows', 'seq')), may hold values from -0.09375 to 0.09375
- down_bias: bfloat16 [1152], P(('rows', 'seq')), may hold values from -3 to 3
- cotangent: bfloat16 [2, 8, 1024, 1152], P(None, 'rows', 'seq'), may hold values from -6 to 6
Outputs:
- block_output: bfloat16 [2, 8, 1024, 1152], P(None, 'rows', 'seq')
- grad_tokens: float32 [2, 8, 1024, 1152], P(None, 'rows', 'seq')
- grad_norm1_gain: float32 [1152], P(('rows', 'seq'))
- grad_norm1_bias: float32 [1152], P(('rows', 'seq'))
- grad_w_query: float32 [1152, 1152], P(('rows', 'seq'))
- grad_query_bias: float32 [1152], P(('rows', 'seq'))
- grad_w_key: float32 [1152, 1152], P(('rows', 'seq'))
- grad_w_value: float32 [1152, 1152], P(('rows', 'seq'))
- grad_value_bias: float32 [1152], P(('rows', 'seq'))
- grad_w_out: float32 [1152, 1152], P(('rows', 'seq'))
- grad_out_bias: float32 [1152], P(('rows', 'seq'))
- grad_norm2_gain: float32 [1152], P(('rows', 'seq'))
- grad_norm2_bias: float32 [1152], P(('rows', 'seq'))
- grad_w_up: float32 [1152, 4304], P(('rows', 'seq'))
- grad_up_bias: float32 [4304], replicated
- grad_w_down: float32 [4304, 1152], P(None, ('rows', 'seq'))
- grad_down_bias: float32 [1152], P(('rows', 'seq'))
The draws below stay inside these ranges and needn't reach their ends.
Inputs may be any that keep to these rules, and one draw needn't show every extreme that they name: In each row the first three entries are picture lengths and the last is the padding run; they sum to 1024; one picture holds the rest of the row, and the two other pictures and the padding run hold at most 64 tokens each.
All inputs are finite; a program needn't handle non-finite values.
Results may differ from the reference program's by a relative error of at most 0.012.
Values may be sent and summed in bfloat16 or wider, within the bound.
No kernel may reach another device: no remote copies, remote signals or barrier semaphores. Data moves between devices by JAX's collectives and lax.ppermute only.
A program may use at most 320 MiB of HBM per device.

```python
import jax
import jax.numpy as jnp
from jax import lax

H = 16
HD = 72
D = 1152
FF = 4304
LENGTH = 1024
MICRO = 2
ROWS = 8
SHORT = 64


def draw_lengths(key, part):
    key = jax.random.fold_in(key, 11)
    key_short, key_padding, key_placed = jax.random.split(key, 3)
    shorts = jax.random.randint(key_short, (MICRO, ROWS, 2), 1, SHORT + 1)
    padding = jax.random.randint(key_padding, (MICRO, ROWS, 1), 1, SHORT + 1)
    longest = LENGTH - jnp.sum(shorts, axis=-1, keepdims=True) - padding
    placed = jax.random.randint(key_placed, (MICRO, ROWS, 1), 0, 3)
    slot_ids = jnp.arange(3, dtype=jnp.int32)[None, None, :]
    chosen = jnp.clip(slot_ids - (slot_ids > placed).astype(jnp.int32), 0, 1)
    short_at = jnp.take_along_axis(shorts, jnp.broadcast_to(chosen, (MICRO, ROWS, 3)), axis=-1)
    pictures = jnp.where(slot_ids == placed, longest, short_at)
    return jnp.concatenate([pictures, padding], axis=-1).astype(jnp.int32)


def steps_of(own_key, shape, cuts, least, largest):
    loudness, own = 1.0, jax.random.fold_in(own_key, 6)
    for axis_at, parts in cuts:
        draws = jnp.exp(jax.random.uniform(jax.random.fold_in(own, axis_at), (parts,), jnp.float32, least / len(cuts), largest / len(cuts)))
        loudness = loudness * jnp.repeat(draws, shape[axis_at] // parts).reshape([-1 if axis == axis_at else 1 for axis in range(len(shape))])
    return loudness


def gaussian(own_key, dims, deviation, limit, cuts=(), held_as=jnp.bfloat16):
    entries = deviation * jax.random.normal(own_key, dims, jnp.float32)
    if cuts:
        entries = entries * steps_of(own_key, dims, cuts, -0.22, 0.18)
    return jnp.clip(entries, -limit, limit).astype(held_as)


def setup_inputs(seed: int = 0) -> dict:
    key_list = jax.random.split(jax.random.key(seed), 19)
    tokens = gaussian(key_list[0], (MICRO, ROWS, LENGTH, D), 1.0, 6.0, ((1, 8), (2, 4)))
    lengths = draw_lengths(jax.random.fold_in(key_list[18], 71), 0)
    norm1_gain = jnp.clip(1.0 + 0.15 * jax.random.normal(key_list[2], (D,), jnp.float32), 0.25, 1.75).astype(jnp.bfloat16)
    norm1_bias = gaussian(key_list[3], (D,), 0.5, 3.0, ((0, 32),))
    w_query = gaussian(key_list[4], (D, D), D ** -0.5, 0.1875, ((0, 32),))
    query_bias = gaussian(key_list[5], (D,), 0.5, 3.0, ((0, 32),))
    w_key = gaussian(key_list[6], (D, D), D ** -0.5, 0.1875, ((0, 32),))
    w_value = gaussian(key_list[7], (D, D), D ** -0.5, 0.1875, ((0, 32),))
    value_bias = gaussian(key_list[8], (D,), 0.5, 3.0, ((0, 32),))
    w_out = gaussian(key_list[9], (D, D), (max(4 * D // LENGTH, 1)) ** -0.5, 3.0, ((0, 32),))
    out_bias = gaussian(key_list[10], (D,), 0.5, 3.0, ((0, 32),))
    norm2_gain = jnp.clip(1.0 + 0.15 * jax.random.normal(key_list[11], (D,), jnp.float32), 0.25, 1.75).astype(jnp.bfloat16)
    norm2_bias = gaussian(key_list[12], (D,), 0.5, 3.0, ((0, 32),))
    w_up = gaussian(key_list[13], (D, FF), D ** -0.5, 0.1875, ((0, 32),))
    up_bias = gaussian(key_list[14], (FF,), 0.5, 3.0)
    w_down = gaussian(key_list[15], (FF, D), FF ** -0.5, 0.09375, ((1, 32),))
    down_bias = gaussian(key_list[16], (D,), 0.5, 3.0, ((0, 32),))
    cotangent = gaussian(key_list[17], (MICRO, ROWS, LENGTH, D), 1.0, 6.0, ((1, 8), (2, 4)))
    return dict(tokens=tokens, lengths=lengths, norm1_gain=norm1_gain, norm1_bias=norm1_bias, w_query=w_query, query_bias=query_bias, w_key=w_key, w_value=w_value, value_bias=value_bias, w_out=w_out, out_bias=out_bias, norm2_gain=norm2_gain, norm2_bias=norm2_bias, w_up=w_up, up_bias=up_bias, w_down=w_down, down_bias=down_bias, cotangent=cotangent)


@jax.custom_vjp
def low(v):
    return lax.optimization_barrier(v.astype(jnp.bfloat16)).astype(jnp.float32)

@jax.custom_vjp
def low_back(v):
    return v

def low_keep(v):
    return (low(v), None)

def low_pass(kept, grad):
    return (grad,)

def back_keep(v):
    return (v, None)

def back_low(kept, grad):
    return (low(grad),)
low.defvjp(low_keep, low_pass)
low_back.defvjp(back_keep, back_low)
highest = lax.Precision.HIGHEST

def rounded(value):
    return low_back(low(value))

def layer_norm(values, gain, shift):
    center = lax.optimization_barrier(jnp.mean(values, axis=-1, keepdims=True))
    centered = values - center
    spread = lax.optimization_barrier(jnp.mean(centered * centered, axis=-1, keepdims=True))
    return centered * lax.rsqrt(spread + 1e-06) * gain + shift

def segment_ids(lengths):
    ends = jnp.cumsum(lengths, axis=-1)
    places = jnp.arange(LENGTH, dtype=jnp.int32)
    return lax.optimization_barrier(jnp.sum((places[:, None] >= ends[..., None, :]).astype(jnp.int32), axis=-1))

def one_row(params, row_tokens, segments):
    gain_one, shift_one, w_query, query_bias, w_key, w_value, value_bias, w_out, out_bias, gain_two, shift_two, w_up, up_bias, w_down, down_bias = params
    normed = low(layer_norm(row_tokens, gain_one, shift_one))
    queries = rounded(jnp.dot(normed, w_query, precision=highest) + query_bias)
    key_rows = rounded(jnp.dot(normed, w_key, precision=highest))
    values = rounded(jnp.dot(normed, w_value, precision=highest) + value_bias)
    query_heads = queries.reshape(LENGTH, H, HD)
    key_heads = key_rows.reshape(LENGTH, H, HD)
    value_heads = values.reshape(LENGTH, H, HD)
    scores = jnp.einsum('qhd,khd->hqk', query_heads, key_heads, precision=highest) * HD ** (-0.5)
    same_picture = segments[:, None] == segments[None, :]
    scores = low_back(jnp.where(same_picture[None], scores, -1e+30))
    attend_weights = low(jax.nn.softmax(scores, axis=-1))
    attended = rounded(jnp.einsum('hqk,khd->qhd', attend_weights, value_heads, precision=highest).reshape(LENGTH, H * HD))
    residual_one = row_tokens + low_back(jnp.dot(attended, w_out, precision=highest) + out_bias)
    normed_two = low(layer_norm(residual_one, gain_two, shift_two))
    hidden = low_back(jnp.dot(normed_two, w_up, precision=highest) + up_bias)
    active = low(jax.nn.gelu(hidden, approximate=True))
    return residual_one + low_back(jnp.dot(active, w_down, precision=highest) + down_bias)

def reference(tokens, lengths, norm1_gain, norm1_bias, w_query, query_bias, w_key, w_value, value_bias, w_out, out_bias, norm2_gain, norm2_bias, w_up, up_bias, w_down, down_bias, cotangent):
    model_width = H * HD
    segments = segment_ids(lengths).reshape(-1, LENGTH).astype(jnp.int32)
    flat_tokens = tokens.astype(jnp.float32).reshape(-1, LENGTH, model_width)
    params = tuple((item.astype(jnp.float32) for item in (norm1_gain, norm1_bias, w_query, query_bias, w_key, w_value, value_bias, w_out, out_bias, norm2_gain, norm2_bias, w_up, up_bias, w_down, down_bias)))

    def forward(all_tokens, weights):
        row_step = jax.checkpoint(lambda pair: one_row(weights, pair[0], pair[1]))
        return lax.map(row_step, (all_tokens, segments))
    output, pull = jax.vjp(forward, flat_tokens, params)
    grad_flat, grads = pull(cotangent.astype(jnp.float32).reshape(-1, LENGTH, model_width))
    block_output = output.reshape(tokens.shape).astype(jnp.bfloat16)
    grad_tokens = grad_flat.reshape(tokens.shape)
    return (block_output, grad_tokens, grads[0], grads[1], grads[2], grads[3], grads[4], grads[5], grads[6], grads[7], grads[8], grads[9], grads[10], grads[11], grads[12], grads[13], grads[14])
```

```python
import functools

import jax
import jax.numpy as jnp
from jax import lax
from jax.experimental import pallas as pl
from jax.experimental.pallas import tpu as pltpu
from jax.sharding import PartitionSpec as P

H = 16
HD = 72
AXES = ("rows", "seq")
norm_epsilon = 1e-06
BIG = 1e30
LANE = 128
WIN = 256
bf16 = jnp.bfloat16
f32 = jnp.float32
NT = (((1,), (1,)), ((), ()))
TN = (((0,), (0,)), ((), ()))
NN = (((1,), (0,)), ((), ()))


def dot(a, b, dims=NN, out=f32):
    return lax.dot_general(a, b, dims, preferred_element_type=f32).astype(out)


class Places:
    def __init__(self, n_rows, n_seq):
        self.nz, self.ny, self.nx, self.nc = n_rows // 2, 2, n_seq // 2, 2
        every = [
            (z, y, x, c)
            for z in range(self.nz)
            for y in range(2)
            for x in range(2)
            for c in range(2)
        ]
        nz = self.nz

        def flat(z, y, x, c):
            return ((z * 2 + y) * 2 + x) * 2 + c

        def pairs(f):
            return [(flat(*t), flat(*f(*t))) for t in every]

        self.to_core = pairs(lambda z, y, x, c: (z, y, x, 1 - c))
        self.to_x = pairs(lambda z, y, x, c: (z, y, 1 - x, c))
        self.to_y = pairs(lambda z, y, x, c: (z, 1 - y, x, c))
        self.to_z = pairs(lambda z, y, x, c: ((z + 1) % nz, y, x, c))
        r, s = lax.axis_index("rows"), lax.axis_index("seq")
        self.z, self.y, self.x, self.c = r // 2, r % 2, s // 2, s % 2


def send(value, pairs):
    return lax.ppermute(value, AXES, pairs)


def place_kernel(n_in, n_dyn, plan, *refs):
    dyn = refs[0]
    ins, out, sem = refs[1 : 1 + n_in], refs[1 + n_in], refs[2 + n_in]
    d = [dyn[i] for i in range(n_dyn)]
    copies = []
    for j, (i, src, dst) in enumerate(plan):
        copies.append(pltpu.make_async_copy(ins[i].at[src], out.at[dst(*d)], sem.at[j]))
    for copy in copies:
        copy.start()
    for copy in copies:
        copy.wait()


def place(at, ins, plan, block):
    rows, cols = block
    dyn = jnp.stack([at.z, at.y, at.x]).astype(jnp.int32)
    shape = (at.nz, 2, 2, rows, cols)
    if rows % 8 == 0:
        out = pl.pallas_call(
            functools.partial(place_kernel, len(ins), 3, plan),
            out_shape=jax.ShapeDtypeStruct(shape, ins[0].dtype),
            in_specs=[pl.BlockSpec(memory_space=pltpu.SMEM)]
            + [pl.BlockSpec(memory_space=pl.ANY)] * len(ins),
            out_specs=pl.BlockSpec(memory_space=pltpu.VMEM),
            scratch_shapes=[pltpu.SemaphoreType.DMA((len(plan),))],
            compiler_params=pltpu.CompilerParams(vmem_limit_bytes=16 * 1024 * 1024),
            cost_estimate=pl.CostEstimate(
                flops=0,
                bytes_accessed=4 * at.nz * 4 * rows * cols,
                transcendentals=0,
            ),
        )(dyn, *ins)
    else:
        out = jnp.zeros(shape, ins[0].dtype)
        for i, src, dst in plan:
            piece = ins[i][src]
            out = lax.dynamic_update_slice(
                out, piece[None, None, None], (*dst(at.z, at.y, at.x), 0, 0)
            )
    return out.reshape(at.nz * 4 * rows, cols)


def ring(at, value):
    held = [value]
    for _ in range(at.nz - 1):
        value = send(value, at.to_z)
        held.append(value)
    return held


def flip(here, by):
    return here + by - 2 * by * here


def gather(at, mine, order):
    rows, cols = mine.shape
    nz = at.nz
    plan = []
    first, second = (at.to_x, at.to_y) if order in ("zxy", "xzy") else (at.to_y, at.to_x)
    x_first = order in ("zxy", "xzy")

    def slot(k, a, b):
        dx, dy = (a, b) if x_first else (b, a)
        return lambda z, y, x: (lax.rem(z - k + nz, nz), flip(y, dy), flip(x, dx))

    if order[0] == "z":
        line = jnp.stack(ring(at, mine))
        one = send(line, first)
        two = send(line, second)
        both = send(one, second)
        ins = [line, one, two, both]
        for i, (a, b) in enumerate(((0, 0), (1, 0), (0, 1), (1, 1))):
            for k in range(nz):
                plan.append((i, (k,), slot(k, a, b)))
    else:
        pair = jnp.stack([mine, send(mine, first)])
        line = ring(at, pair)
        ins = line + [send(v, second) for v in line]
        for b in range(2):
            for k in range(nz):
                for a in range(2):
                    plan.append((b * nz + k, (a,), slot(k, a, b)))
    return place(at, ins, plan, (rows, cols))


def relative_order(at, order, chip_rows, width):
    nz = at.nz
    place_of = jnp.arange(width, dtype=jnp.int32)
    block, row = place_of // chip_rows, place_of % chip_rows
    if order == "yzx":
        b, k, a = block // (2 * nz), (block // 2) % nz, block % 2
    elif order == "xzy":
        a, k, b = block // (2 * nz), (block // 2) % nz, block % 2
    elif order == "yxz":
        b, a, k = block // (2 * nz), (block // nz) % 2, block % nz
    else:
        a, b, k = block // (2 * nz), (block // nz) % 2, block % nz
    z = (at.z - 1 - k + 2 * nz) % nz
    natural = ((z * 2 + flip(at.y, b)) * 2 + flip(at.x, a)) * chip_rows + row
    return (jnp.arange(width, dtype=jnp.int32)[:, None] == natural[None, :]).astype(bf16)


def scatter(at, left_own, right_own, left_peer, right_peer, order):
    width = left_own.shape[1]
    n = right_own.shape[1]
    half = width // 2
    first = at.to_y if order[0] == "y" else at.to_x
    from_core = send(dot(left_peer, right_peer, TN, bf16), at.to_core)
    going = (dot(left_own[:, half:], right_own, TN) + from_core[half:].astype(f32)).astype(bf16)
    came = send(going, first)
    kept = (
        dot(left_own[:, :half], right_own, TN)
        + from_core[:half].astype(f32)
        + came.astype(f32)
    ).astype(bf16)
    if order[2] == "z":
        second = at.to_x if order[1] == "x" else at.to_y
        quarter = half // 2
        kept = (
            kept[:quarter].astype(f32) + send(kept[quarter:], second).astype(f32)
        ).astype(bf16)
        kept = kept.reshape(at.nz, quarter // at.nz, n)
        total = kept[0]
        for k in range(1, at.nz):
            total = send(total.astype(bf16), at.to_z).astype(f32) + kept[k].astype(f32)
    else:
        second = at.to_x if order[2] == "x" else at.to_y
        kept = kept.reshape(at.nz, 2, half // at.nz // 2, n)
        total = kept[0]
        for k in range(1, at.nz):
            total = send(total.astype(bf16), at.to_z).astype(f32) + kept[k].astype(f32)
        total = total[0] + send(total[1].astype(bf16), second).astype(f32)
    rows = total.shape[0] // 2
    mine = jnp.where(at.c == 0, total[:rows], total[rows:])
    theirs = jnp.where(at.c == 0, total[rows:], total[:rows])
    return mine, send(theirs, at.to_core)


def window(h):
    tile = jnp.minimum((h * HD) // LANE, (H * HD - WIN) // LANE)
    start = pl.multiple_of(tile * LANE, LANE)
    return start, h * HD - start


def head_masks(h, rows):
    start, off = window(h)
    lane = lax.broadcasted_iota(jnp.int32, (rows, WIN), 1)
    inside = (lane >= off) & (lane < off + HD)
    at = jnp.where(off > WIN - HD - 4, 0, WIN - 4)
    feature = (lane >= at) & (lane < at + 4)
    return start, inside, feature


def attend_kernel(q_ref, ko_ref, kr_ref, vo_ref, vr_ref, qf_ref, kf_ref, out_ref, lse_ref, acc):
    t, n = q_ref.shape[0], ko_ref.shape[0]
    acc[...] = jnp.zeros_like(acc)
    scale = (HD ** -0.5) * 1.4426950408889634
    zero = jnp.zeros((), bf16)

    def head(h, carry):
        start, in_k, feat_k = head_masks(h, n)
        _, _, feat_q = head_masks(h, t)
        at = pl.ds(start, WIN)
        q = jnp.where(feat_q, qf_ref[...], q_ref[:, at])
        keys, vals = [], []
        for i, (kref, vref) in enumerate(((ko_ref, vo_ref), (kr_ref, vr_ref))):
            feats = jnp.where(feat_k, kf_ref[i * n : (i + 1) * n, :], zero)
            keys.append(jnp.where(in_k, kref[:, at], feats))
            vals.append(jnp.where(in_k, vref[:, at], zero))
        k = jnp.concatenate(keys, axis=0)
        v_t = jnp.concatenate(vals, axis=0).T
        s = lax.dot_general(k, q, NT, preferred_element_type=f32)
        top = jnp.max(s, axis=0, keepdims=True) * scale
        p = jnp.exp2(s * scale - top)
        total = jnp.sum(p, axis=0, keepdims=True)
        o_t = lax.dot_general(v_t, p.astype(bf16), NN, preferred_element_type=f32)
        acc[:, at] += (o_t / total).T
        lse_ref[pl.ds(h, 1), :] = top + jnp.log2(total)
        return carry

    lax.fori_loop(0, H, head, 0)
    out_ref[...] = acc[...].astype(bf16)


def attend(q, ko, kr, vo, vr, qf, kf):
    t, d = q.shape
    return pl.pallas_call(
        attend_kernel,
        out_shape=(
            jax.ShapeDtypeStruct((t, d), bf16),
            jax.ShapeDtypeStruct((H, t), f32),
        ),
        scratch_shapes=[pltpu.VMEM((t, d), f32)],
        compiler_params=pltpu.CompilerParams(vmem_limit_bytes=48 * 1024 * 1024),
        cost_estimate=pl.CostEstimate(
            flops=4 * H * t * 2 * t * WIN, bytes_accessed=12 * t * d, transcendentals=H * t * 2 * t
        ),
    )(q, ko, kr, vo, vr, qf, kf)


def back_kernel(
    q_ref, ko_ref, kr_ref, vo_ref, vr_ref, do_ref, qf_ref, kf_ref, lse_ref,
    dq_ref, dko_ref, dvo_ref, dkr_ref, dvr_ref, dq, dk, dv,
):
    t, n = q_ref.shape[0], ko_ref.shape[0]
    scale = HD ** -0.5
    scale_two = scale * 1.4426950408889634
    zero = jnp.zeros((), bf16)
    dq[...] = jnp.zeros_like(dq)
    dk[...] = jnp.zeros_like(dk)
    dv[...] = jnp.zeros_like(dv)

    def head(h, carry):
        start, in_k, feat_k = head_masks(h, n)
        _, in_q, feat_q = head_masks(h, t)
        at = pl.ds(start, WIN)
        q_win = q_ref[:, at]
        q = jnp.where(feat_q, qf_ref[...], q_win)
        q_only = jnp.where(in_q, q_win, zero)
        do = jnp.where(in_q, do_ref[:, at], zero)
        keys, vals, only = [], [], []
        for i, (kref, vref) in enumerate(((ko_ref, vo_ref), (kr_ref, vr_ref))):
            feats = jnp.where(feat_k, kf_ref[i * n : (i + 1) * n, :], zero)
            k_win = kref[:, at]
            keys.append(jnp.where(in_k, k_win, feats))
            only.append(jnp.where(in_k, k_win, zero))
            vals.append(vref[:, at])
        k = jnp.concatenate(keys, axis=0)
        k_t = jnp.concatenate(only, axis=0).T
        v = jnp.concatenate(vals, axis=0)
        s = lax.dot_general(k, q, NT, preferred_element_type=f32)
        p = jnp.exp2(s * scale_two - lse_ref[pl.ds(h, 1), :])
        dp = lax.dot_general(v, do, NT, preferred_element_type=f32)
        dv[:, at] += lax.dot_general(p.astype(bf16), do, NN, preferred_element_type=f32)
        inner = jnp.sum(p * dp, axis=0, keepdims=True)
        ds = (p * (dp - inner)).astype(bf16)
        dk[:, at] += lax.dot_general(ds, q_only, NN, preferred_element_type=f32)
        dq[:, at] += lax.dot_general(k_t, ds, NN, preferred_element_type=f32).T
        return carry

    lax.fori_loop(0, H, head, 0)
    dq_ref[...] = (dq[...] * scale).astype(bf16)
    dko_ref[...] = (dk[:n, :] * scale).astype(bf16)
    dkr_ref[...] = (dk[n:, :] * scale).astype(bf16)
    dvo_ref[...] = dv[:n, :].astype(bf16)
    dvr_ref[...] = dv[n:, :].astype(bf16)


def attend_back(q, ko, kr, vo, vr, do, qf, kf, lse):
    t, d = q.shape
    n = ko.shape[0]
    return pl.pallas_call(
        back_kernel,
        out_shape=(jax.ShapeDtypeStruct((t, d), bf16),)
        + (jax.ShapeDtypeStruct((n, d), bf16),) * 4,
        scratch_shapes=[
            pltpu.VMEM((t, d), f32),
            pltpu.VMEM((2 * n, d), f32),
            pltpu.VMEM((2 * n, d), f32),
        ],
        compiler_params=pltpu.CompilerParams(vmem_limit_bytes=60 * 1024 * 1024),
        cost_estimate=pl.CostEstimate(
            flops=10 * H * t * 2 * n * WIN,
            bytes_accessed=24 * t * d,
            transcendentals=H * t * 2 * n,
        ),
    )(q, ko, kr, vo, vr, do, qf, kf, lse)


def norm_parts(values):
    center = jnp.mean(values, axis=-1, keepdims=True)
    centered = values - center
    spread = jnp.mean(centered * centered, axis=-1, keepdims=True)
    inverse = lax.rsqrt(spread + norm_epsilon)
    return centered * inverse, inverse


def norm_back(incoming, gain, unit, inverse):
    scaled = incoming * gain
    return (
        scaled
        - jnp.mean(scaled, axis=-1, keepdims=True)
        - unit * jnp.mean(scaled * unit, axis=-1, keepdims=True)
    ) * inverse


def column_sum(rows):
    return jnp.sum(rows.astype(f32), axis=0)


def gelu_and_slope(z):
    root = 0.7978845608028654
    cube = 0.044715
    t = jnp.tanh(root * (z + cube * z * z * z))
    value = 0.5 * z * (1.0 + t)
    slope = 0.5 * (1.0 + t) + 0.5 * z * (1.0 - t * t) * root * (1.0 + 3.0 * cube * z * z)
    return value, slope


def lane_cut(width):
    tiles = width // LANE
    one = (tiles * 65) // 100
    return one * LANE


def on_device(
    tokens,
    lengths,
    norm1_gain,
    norm1_bias,
    w_query,
    query_bias,
    w_key,
    w_value,
    value_bias,
    w_out,
    out_bias,
    norm2_gain,
    norm2_bias,
    w_up,
    up_bias,
    w_down,
    down_bias,
    cotangent,
):
    at = Places(lax.axis_size("rows"), lax.axis_size("seq"))
    micro, rows_here, local_len, width = tokens.shape
    full_len = local_len * lax.axis_size("seq")
    own_rows, hidden_width = w_up.shape
    chip_rows = 2 * own_rows
    zero_core = at.c == 0

    def by_core(a, b):
        return jnp.where(zero_core, a, b)

    vectors = jnp.stack(
        [norm1_gain, norm1_bias, query_bias, value_bias, out_bias, norm2_gain, norm2_bias, down_bias]
    )
    vectors = lax.all_gather(vectors, AXES, axis=0)
    vectors = jnp.swapaxes(vectors, 0, 1).reshape(8, width).astype(f32)
    gain_one, shift_one, bias_q, bias_v, bias_o, gain_two, shift_two, bias_d = [
        vectors[i][None] for i in range(8)
    ]

    def swap_in(values):
        mine = lax.dynamic_index_in_dim(values, at.x, 0, keepdims=False)
        theirs = lax.dynamic_index_in_dim(values, 1 - at.x, 0, keepdims=False)
        came = send(theirs, at.to_x)
        low = jnp.where(at.x == 0, mine, came)
        high = jnp.where(at.x == 0, came, mine)
        return jnp.stack([low, high]).reshape(2 * rows_here * local_len, width)

    def swap_out(values):
        values = values.reshape(2, rows_here, local_len, width)
        mine = lax.dynamic_index_in_dim(values, at.x, 0, keepdims=False)
        theirs = lax.dynamic_index_in_dim(values, 1 - at.x, 0, keepdims=False)
        came = send(theirs.astype(bf16), at.to_x).astype(mine.dtype)
        return jnp.stack([jnp.where(at.x == 0, mine, came), jnp.where(at.x == 0, came, mine)])

    half_width = -(-hidden_width // (2 * LANE)) * LANE
    cut = lane_cut(half_width)
    up_full = jnp.pad(w_up, ((0, 0), (0, 2 * half_width - hidden_width)))
    eye = jnp.eye(own_rows, dtype=bf16)
    down_t = dot(eye, w_down, NT, bf16)
    down_full = jnp.pad(down_t, ((0, 0), (0, 2 * half_width - hidden_width)))
    low = [w_query, w_key, up_full[:, :half_width], down_full[:, :half_width]]
    high = [w_value, w_out, up_full[:, half_width:], down_full[:, half_width:]]
    low, high = jnp.concatenate(low, axis=1), jnp.concatenate(high, axis=1)
    keep, give = by_core(low, high), by_core(high, low)
    both = jnp.concatenate([keep, send(give, at.to_core)], axis=0)
    spot = jnp.arange(chip_rows, dtype=jnp.int32)
    spot = flip(at.c, spot // own_rows) * own_rows + spot % own_rows
    turn = (jnp.arange(chip_rows, dtype=jnp.int32)[:, None] == spot[None, :]).astype(bf16)
    ends = [0, width, 2 * width]
    ends += [ends[-1] + cut, ends[-1] + half_width]
    ends += [ends[-1] + cut, ends[-1] + half_width]
    shards = [dot(turn, both[:, a:b], NN, bf16) for a, b in zip(ends[:-1], ends[1:])]
    x_in = swap_in(tokens)
    grad_out = swap_in(cotangent)

    orders = ["zxy", "zyx", "xzy", "yzx", "xzy", "yzx"]
    own = [gather(at, s, o) for s, o in zip(shards, orders)]
    other = [send(w, at.to_core) for w in own]
    weight_q, weight_v = by_core(own[0], other[0]), by_core(other[0], own[0])
    weight_k, weight_o = by_core(own[1], other[1]), by_core(other[1], own[1])
    up_parts = [own[2], own[3], other[2], other[3]]
    down_parts = [own[4], own[5], other[4], other[5]]
    bias_up = jnp.pad(up_bias.astype(f32), (0, 2 * half_width - hidden_width))
    bias_own = by_core(bias_up[:half_width], bias_up[half_width:])
    bias_other = by_core(bias_up[half_width:], bias_up[:half_width])
    bias_parts = [bias_own[:cut], bias_own[cut:], bias_other[:cut], bias_other[cut:]]

    row_lengths = lax.dynamic_index_in_dim(lengths, at.x, 0, keepdims=False)[0]
    ends_at = jnp.cumsum(row_lengths)
    inside = jnp.arange(2 * local_len, dtype=jnp.int32)
    def segment_of(core):
        spots = (inside // local_len) * (full_len // 2) + core * local_len + inside % local_len
        return jnp.sum((spots[:, None] >= ends_at[None, :]).astype(jnp.int32), axis=-1)
    seg_own, seg_other = segment_of(at.c), segment_of(1 - at.c)
    lane = (jnp.arange(WIN, dtype=jnp.int32) % 4)[None, :]
    feat_q = (seg_own[:, None] == lane).astype(bf16)
    seg_keys = jnp.concatenate([seg_own, seg_other])
    feat_k = jnp.where(seg_keys[:, None] == lane, 0.0, -BIG).astype(bf16)

    inputs = x_in.astype(f32)
    unit_one, inverse_one = norm_parts(inputs)
    normed = (unit_one * gain_one + shift_one).astype(bf16)
    queries = (dot(normed, weight_q) + bias_q).astype(bf16)
    keys = dot(normed, weight_k, NN, bf16)
    values = (dot(normed, weight_v) + bias_v).astype(bf16)
    keys_other, values_other = send(keys, at.to_core), send(values, at.to_core)
    attended, lse = attend(queries, keys, keys_other, values, values_other, feat_q, feat_k)
    residual_one = inputs + dot(attended, weight_o) + bias_o
    unit_two, inverse_two = norm_parts(residual_one)
    normed_two = (unit_two * gain_two + shift_two).astype(bf16)
    active, slopes = [], []
    for w, b in zip(up_parts, bias_parts):
        value, slope = gelu_and_slope(dot(normed_two, w) + b[None])
        active.append(value.astype(bf16))
        slopes.append(slope.astype(bf16))
    result = residual_one + bias_d
    for a, w in zip(active, down_parts):
        result = result + dot(a, w, NT)
    block_output = swap_out(result.astype(bf16))

    order_y = relative_order(at, "yzx", chip_rows, width)
    order_x = relative_order(at, "xzy", chip_rows, width)
    order_one = relative_order(at, "yxz", chip_rows, width)
    order_two = relative_order(at, "xyz", chip_rows, width)
    out_y, out_x = dot(grad_out, order_y, NN, bf16), dot(grad_out, order_x, NN, bf16)
    d_down = [
        scatter(at, out_y, active[0], out_y, active[2], "yzx"),
        scatter(at, out_x, active[1], out_x, active[3], "xzy"),
    ]
    grad_hidden = [
        (dot(grad_out, w) * s.astype(f32)).astype(bf16) for w, s in zip(down_parts, slopes)
    ]
    two_y, two_x = dot(normed_two, order_y, NN, bf16), dot(normed_two, order_x, NN, bf16)
    d_up = [
        scatter(at, two_y, grad_hidden[0], two_y, grad_hidden[2], "yzx"),
        scatter(at, two_x, grad_hidden[1], two_x, grad_hidden[3], "xzy"),
    ]
    grad_normed_two = dot(grad_hidden[0], up_parts[0], NT)
    for g, w in zip(grad_hidden[1:], up_parts[1:]):
        grad_normed_two = grad_normed_two + dot(g, w, NT)
    grad_residual = grad_out.astype(f32) + norm_back(
        grad_normed_two, gain_two, unit_two, inverse_two
    )
    grad_branch = grad_residual.astype(bf16)
    grad_attended = dot(grad_branch, weight_o, NT, bf16)
    grad_q, gko, gvo, gkr, gvr = attend_back(
        queries, keys, keys_other, values, values_other, grad_attended, feat_q, feat_k, lse
    )
    grad_k = (gko.astype(f32) + send(gkr, at.to_core).astype(f32)).astype(bf16)
    grad_v = (gvo.astype(f32) + send(gvr, at.to_core).astype(f32)).astype(bf16)
    one = dot(normed, order_one, NN, bf16)
    two = dot(normed, order_two, NN, bf16)
    attended_two = dot(attended, order_two, NN, bf16)
    d_qv = scatter(at, one, by_core(grad_q, grad_v), one, by_core(grad_v, grad_q), "yxz")
    d_ko = scatter(
        at,
        by_core(two, attended_two),
        by_core(grad_k, grad_branch),
        by_core(attended_two, two),
        by_core(grad_branch, grad_k),
        "xyz",
    )
    grad_normed = (
        dot(grad_q, weight_q, NT) + dot(grad_k, weight_k, NT) + dot(grad_v, weight_v, NT)
    )
    grad_tokens = grad_residual + norm_back(grad_normed, gain_one, unit_one, inverse_one)
    grad_tokens = swap_out(grad_tokens)

    hidden_sums = [column_sum(g) for g in grad_hidden]
    own_sums = jnp.concatenate(hidden_sums[:2])
    other_sums = jnp.concatenate(hidden_sums[2:])
    up_sums = jnp.concatenate([by_core(own_sums, other_sums), by_core(other_sums, own_sums)])
    early = jnp.concatenate(
        [
            column_sum(grad_out),
            column_sum(grad_branch),
            column_sum(grad_normed_two * unit_two),
            column_sum(grad_normed_two),
            up_sums,
        ]
    )
    late = jnp.concatenate(
        [
            column_sum(grad_q),
            column_sum(grad_v),
            column_sum(grad_normed * unit_one),
            column_sum(grad_normed),
        ]
    )
    early = lax.psum(early, AXES)
    late = lax.psum(late, AXES)
    my_start = (lax.axis_index("rows") * lax.axis_size("seq") + lax.axis_index("seq")) * own_rows

    def my_part(vector, i):
        return lax.dynamic_slice_in_dim(vector, i * width + my_start, own_rows)

    d_up_bias = early[4 * width : 4 * width + hidden_width]

    def halves(parts):
        mine = jnp.concatenate([p[0] for p in parts], axis=1)
        theirs = jnp.concatenate([p[1] for p in parts], axis=1)
        both = jnp.concatenate([by_core(mine, theirs), by_core(theirs, mine)], axis=1)
        return both[:, :hidden_width]

    d_w_up = halves(d_up)
    d_w_down = halves(d_down).T
    return (
        block_output,
        grad_tokens,
        my_part(late, 2),
        my_part(late, 3),
        by_core(d_qv[0], d_qv[1]),
        my_part(late, 0),
        by_core(d_ko[0], d_ko[1]),
        by_core(d_qv[1], d_qv[0]),
        my_part(late, 1),
        by_core(d_ko[1], d_ko[0]),
        my_part(early, 1),
        my_part(early, 2),
        my_part(early, 3),
        d_w_up,
        d_up_bias,
        d_w_down,
        my_part(early, 0),
    )


def solution(mesh):
    feature = P(AXES)
    matrix = P(AXES, None)
    row = P(None, "rows", "seq", None)
    return jax.shard_map(
        on_device,
        mesh=mesh,
        in_specs=(
            row,
            P(None, "rows", None),
            feature,
            feature,
            matrix,
            feature,
            matrix,
            matrix,
            feature,
            matrix,
            feature,
            feature,
            feature,
            matrix,
            P(),
            P(None, AXES),
            feature,
            row,
        ),
        out_specs=(
            row,
            row,
            feature,
            feature,
            matrix,
            feature,
            matrix,
            matrix,
            feature,
            matrix,
            feature,
            feature,
            feature,
            matrix,
            P(),
            P(None, AXES),
            feature,
        ),
        check_vma=False,
    )
```

```python
import functools

import jax
import jax.numpy as jnp
from jax import lax
from jax.experimental import pallas as pl
from jax.experimental.pallas import tpu as pltpu
from jax.sharding import PartitionSpec as P

H = 16
HD = 72
AXES = ("rows", "seq")
norm_epsilon = 1e-06
BIG = 1e30
LANE = 128
WIN = 256
bf16 = jnp.bfloat16
f32 = jnp.float32
COST = pl.CostEstimate(flops=5 * 10**9, bytes_accessed=10**7, transcendentals=10**6)
NT = (((1,), (1,)), ((), ()))
TN = (((0,), (0,)), ((), ()))
NN = (((1,), (0,)), ((), ()))


def dot(a, b, dims=NN, out=f32):
    return lax.dot_general(a, b, dims, preferred_element_type=f32).astype(out)


class Places:
    def __init__(self, n_rows, n_seq):
        self.nz, self.ny, self.nx, self.nc = n_rows // 2, 2, n_seq // 2, 2
        every = [
            (z, y, x, c)
            for z in range(self.nz)
            for y in range(2)
            for x in range(2)
            for c in range(2)
        ]
        nz = self.nz

        def flat(z, y, x, c):
            return ((z * 2 + y) * 2 + x) * 2 + c

        def pairs(f):
            return [(flat(*t), flat(*f(*t))) for t in every]

        self.to_core = pairs(lambda z, y, x, c: (z, y, x, 1 - c))
        self.to_x = pairs(lambda z, y, x, c: (z, y, 1 - x, c))
        self.to_y = pairs(lambda z, y, x, c: (z, 1 - y, x, c))
        self.to_z = pairs(lambda z, y, x, c: ((z + 1) % nz, y, x, c))
        assert nz & (nz - 1) == 0
        self.z_swaps = [
            pairs(lambda z, y, x, c, bit=1 << i: (z ^ bit, y, x, c))
            for i in range(nz.bit_length() - 1)
        ]
        r, s = lax.axis_index("rows"), lax.axis_index("seq")
        self.z, self.y, self.x, self.c = r // 2, r % 2, s // 2, s % 2


def send(value, pairs):
    return lax.ppermute(value, AXES, pairs)


class Going:
    def __init__(self, value):
        self.value, self.here = value, False


class Line:
    def __init__(self):
        self.token = jnp.zeros((8, LANE), f32)
        self.queue = []

    def pin(self, *values):
        return lax.optimization_barrier((values, self.token))[0]

    def close(self, *values):
        values, self.token = lax.optimization_barrier((values, self.token))
        return values if len(values) > 1 else values[0]

    def done(self, *going):
        while not all(g.here for g in going):
            first = self.queue.pop(0)
            first.value, first.here = self.close(first.value), True
        return [g.value for g in going] if len(going) > 1 else going[0].value

    def run(self, step, *values):
        out = step(*self.pin(*values))
        return self.close(*out) if isinstance(out, tuple) else self.close(out)

    def start(self, value, pairs):
        self.queue.append(Going(send(self.pin(value)[0], pairs)))
        return self.queue[-1]


def flip(here, by):
    return here + by - 2 * by * here


def place_kernel(n_in, n_out, plan, *refs):
    dyn = refs[0]
    ins, outs, sem = refs[1 : 1 + n_in], refs[1 + n_in : 1 + n_in + n_out], refs[1 + n_in + n_out]
    nz = outs[0].shape[0]
    copies = []
    for j, (i, src, src_col, out, dst, dst_col, wide) in enumerate(plan):
        zi, yi, xi = dst(dyn[0], dyn[1], dyn[2])
        zi = lax.rem(zi + dyn[3 + out], nz)
        source = ins[i].at[(*src, slice(None), pl.ds(src_col, wide))]
        target = outs[out].at[zi, yi, xi, :, pl.ds(dst_col, wide)]
        copies.append(pltpu.make_async_copy(source, target, sem.at[j]))
    for copy in copies:
        copy.start()
    for copy in copies:
        copy.wait()


def place(at, ins, plan, rows, widths, turned):
    turns = [jnp.where(at.c == 1, at.nz // 2 if t else 0, 0) for t in turned]
    cut_plan = []
    for i, src, src_col, dst, col, wide in plan:
        left = 0
        for out, out_wide in enumerate(widths):
            low, high = max(col, left), min(col + wide, left + out_wide)
            if low < high:
                cut_plan.append((i, src, src_col + low - col, out, dst, low - left, high - low))
            left += out_wide
    shapes = [(at.nz, 2, 2, rows, w) for w in widths]
    if rows % 8 == 0:
        dyn = jnp.stack([at.z, at.y, at.x, *turns]).astype(jnp.int32)
        outs = pl.pallas_call(
            functools.partial(place_kernel, len(ins), len(widths), cut_plan),
            out_shape=[jax.ShapeDtypeStruct(shape, ins[0].dtype) for shape in shapes],
            in_specs=[pl.BlockSpec(memory_space=pltpu.SMEM)]
            + [pl.BlockSpec(memory_space=pl.ANY)] * len(ins),
            out_specs=[pl.BlockSpec(memory_space=pltpu.VMEM)] * len(widths),
            scratch_shapes=[pltpu.SemaphoreType.DMA((len(cut_plan),))],
            compiler_params=pltpu.CompilerParams(vmem_limit_bytes=16 * 1024 * 1024),
            cost_estimate=COST,
        )(dyn, *ins)
    else:
        outs = [jnp.zeros(shape, ins[0].dtype) for shape in shapes]
        for i, src, src_col, out, dst, dst_col, wide in cut_plan:
            piece = ins[i][src][:, src_col : src_col + wide]
            zi, yi, xi = dst(at.z, at.y, at.x)
            zi = (zi + turns[out]) % at.nz
            outs[out] = lax.dynamic_update_slice(
                outs[out], piece[None, None, None], (zi, yi, xi, 0, dst_col)
            )
    return tuple(o.reshape(at.nz * 4 * rows, w) for o, w in zip(outs, widths))


class Pieces:
    def __init__(self, at, rows, cols):
        self.at, self.rows, self.cols = at, rows, cols
        self.arrays, self.plan = [], []

    def add(self, array, places):
        i, nz = len(self.arrays), self.at.nz
        self.arrays.append(array)
        for index, src_col, (k, dx, dy), col, wide in places:

            def slot(z, y, x, k=k, dx=dx, dy=dy):
                return lax.rem(z - k + nz, nz), flip(y, dy), flip(x, dx)

            self.plan.append((i, index, src_col, slot, col, wide))

    def place(self, line, widths, turned=(False, False)):
        return line.run(
            lambda *v: place(self.at, v, self.plan, self.rows, widths, turned[: len(widths)]),
            *self.arrays,
        )


def pick(values, i, axis=0):
    return lax.dynamic_index_in_dim(values, i, axis, keepdims=False)


class Scatter:
    def __init__(self, line, at, cut, pairs, ends=()):
        self.line, self.at, self.cut, self.pairs = line, at, cut, pairs
        self.ends = ends
        self.ring_at = 0
        self.total = self.low = self.high = self.extra = self.extra_came = None

    def blocks(self, total):
        at = self.at
        return total.reshape(at.nz, 2, 2, 2 * at.own_rows, total.shape[1])

    def cut_out(self, total):
        at, cut = self.at, self.cut
        self.whole = total
        self.low, self.high = [], []

        def step(total):
            v = self.blocks(total)
            low, high = pick(v[..., :cut], 1 - at.y, 1), pick(v[..., cut:], 1 - at.x, 2)
            ends = [0, *self.ends, at.nz]
            return tuple(v[i:j] for v in (low, high) for i, j in zip(ends[:-1], ends[1:]))

        self.parts = list(self.line.run(step, total))

    def begin(self):
        n = len(self.ends) + 1
        i = len(self.low)
        self.low.append(self.line.start(self.parts[i], self.at.to_y))
        self.high.append(self.line.start(self.parts[n + i], self.at.to_x))

    def more(self, total):
        self.extra = total
        part = self.line.run(lambda v: pick(self.blocks(v), 1 - self.at.x, 2), total)
        self.extra_came = self.line.start(part, self.at.to_x)

    def first_of(self, kept):
        return kept, pick(kept, (self.at.z - 1 + self.at.nz) % self.at.nz)

    def arrive(self):
        for going in (self.total, self.low, self.high, self.extra_came):
            if isinstance(going, Going):
                self.line.done(going)
            elif isinstance(going, list):
                self.line.done(*going)

    def keep_run(self):
        at, cut = self.at, self.cut
        came = self.line.done(*self.low, *self.high)
        n = len(self.low)
        extra = () if self.extra is None else (self.extra, self.line.done(self.extra_came))

        def step(total, *came):
            low, high = jnp.concatenate(came[:n]), jnp.concatenate(came[n : 2 * n])
            v = self.blocks(total)
            low = pick(v[..., :cut], at.y, 1).astype(f32) + low.astype(f32)
            high = pick(v[..., cut:], at.x, 2).astype(f32) + high.astype(f32)
            parts = [low, high]
            if extra:
                mine, other = came[2 * n :]
                parts.append(pick(self.blocks(mine), at.x, 2).astype(f32) + other.astype(f32))
            parts = [p.astype(bf16) for p in parts]
            if self.pairs:
                return self.first_of(jnp.concatenate(parts, axis=-1))
            low, high = parts
            return (
                pick(low, at.x, 1), pick(high, at.y, 1),
                pick(low, 1 - at.x, 1), pick(high, 1 - at.y, 1),
            )

        self.kept = self.line.run(step, self.whole, *came, *extra)
        self.whole = self.extra = self.extra_came = self.low = self.high = None

    def keep_start(self):
        kept = self.kept
        if self.pairs:
            self.kept = kept[0]
            self.total = self.line.start(kept[1], self.at.to_z)
        else:
            self.kept = kept[:2]
            self.low = self.line.start(kept[2], self.at.to_x)
            self.high = self.line.start(kept[3], self.at.to_y)

    def keep(self):
        self.keep_run()
        self.keep_start()

    def second(self):
        low, high = self.line.done(self.low, self.high)

        def step(kept_low, kept_high, low, high):
            low = (kept_low.astype(f32) + low.astype(f32)).astype(bf16)
            high = (kept_high.astype(f32) + high.astype(f32)).astype(bf16)
            return self.first_of(jnp.concatenate([low, high], axis=-1))

        self.kept, first = self.line.run(step, *self.kept, low, high)
        self.total = self.line.start(first, self.at.to_z)

    def ring(self):
        at, cut, k = self.at, self.cut, self.ring_at
        if k == at.nz - 1:
            return
        self.ring_at += 1
        last = self.ring_at == at.nz - 1

        def step(total, kept):
            total = total.astype(f32) + pick(kept, (at.z - 2 - k + at.nz) % at.nz).astype(f32)
            if not last:
                return total.astype(bf16)
            if self.pairs:
                low, high = total[..., :cut], total[..., cut:]
                return (
                    jnp.concatenate([pick(low, at.x), pick(high, at.y)], axis=-1),
                    pick(low, 1 - at.x).astype(bf16),
                    pick(high, 1 - at.y).astype(bf16),
                )
            return total

        came = self.line.done(self.total)
        total = self.line.run(step, came, self.kept)
        if not last:
            self.total = self.line.start(total, at.to_z)
        elif self.pairs:
            self.total, self.low, self.high = total
        else:
            self.total = total

    def last_step(self):
        for _ in range(self.at.nz):
            self.ring()

    def last_start(self):
        self.last_step()
        self.low = self.line.start(self.low, self.at.to_x)
        self.high = self.line.start(self.high, self.at.to_y)

    def last(self):
        rows = self.at.own_rows
        self.last_step()

        def step(total, *came):
            if came:
                total = total + jnp.concatenate(came, axis=-1).astype(f32)
            low, high = total[:rows], total[rows:]
            return jnp.where(self.at.c == 0, low, high), jnp.where(self.at.c == 0, high, low)

        came = self.line.done(self.low, self.high) if self.pairs else ()
        self.mine, theirs = self.line.run(step, self.total, *came)
        self.theirs = self.line.start(theirs, self.at.to_core)

    def result(self):
        theirs = self.line.done(self.theirs)
        return (
            jnp.where(self.at.c == 0, self.mine, theirs),
            jnp.where(self.at.c == 0, theirs, self.mine),
        )


class Sums:
    def __init__(self, line, at, value):
        self.line, self.value = line, value
        self.steps = [at.to_core, at.to_x, at.to_y] + at.z_swaps
        self.going = None

    def step(self):
        if self.going is not None:
            came = self.line.done(self.going)
            self.value = self.line.run(lambda v, c: v + c, self.value, came)
        self.going = self.line.start(self.value, self.steps.pop(0)) if self.steps else None

    def result(self):
        while self.going is not None:
            self.step()
        return self.value


CHUNK = 512


def window(h, wide):
    start = pl.multiple_of(jnp.minimum((h * HD) // LANE, (wide - WIN) // LANE) * LANE, LANE)
    return start, h * HD - start


def lane_masks(off, rows):
    lane = lax.broadcasted_iota(jnp.int32, (rows, WIN), 1)
    return (lane >= off) & (lane < off + HD), lane >= WIN - 4


def attend_kernel(first, last, wide, qkv_ref, qf_ref, kf_ref, old_ref, old_lse, out_ref, lse_ref):
    n = qkv_ref.shape[0]
    scale = (HD ** -0.5) * 1.4426950408889634
    zero = jnp.zeros((), bf16)
    if first == 0:
        out_ref[...] = jnp.zeros_like(out_ref)
    else:
        lse_ref[...] = old_lse[...]
        out_ref[...] = old_ref[...]

    def head(h, carry):
        start, off = window(h, wide)
        inside, feature = lane_masks(off, n)
        at = pl.ds(start, WIN)
        k = qkv_ref[:, pl.ds(start + wide, WIN)]
        k = jnp.where(inside, k, jnp.where(feature, kf_ref[...], zero))
        v_t = jnp.where(inside, qkv_ref[:, pl.ds(start + 2 * wide, WIN)], zero).T
        for i in range(n // CHUNK):
            rows = slice(i * CHUNK, (i + 1) * CHUNK)
            q = jnp.where(feature[:CHUNK], qf_ref[rows, :], qkv_ref[rows, at])
            s = lax.dot_general(k, q, NT, preferred_element_type=f32)
            top = jnp.max(s, axis=0, keepdims=True) * scale
            p = jnp.exp2(s * scale - top)
            total = jnp.sum(p, axis=0, keepdims=True)
            o_t = lax.dot_general(v_t, p.astype(bf16), NN, preferred_element_type=f32)
            out = (o_t / total).T.astype(bf16)
            out_ref[rows, at] = jnp.where(inside[:CHUNK], out, out_ref[rows, at])
            lse_ref[pl.ds(h, 1), rows] = top + jnp.log2(total)
        return carry

    lax.fori_loop(first, last, head, 0)


def attend(first, last, qkv, qf, kf, *old):
    n, wide = qkv.shape[0], qkv.shape[1] // 3
    heads = H // 2
    if not old:
        old = (jnp.zeros((16, LANE), bf16), jnp.zeros((8, LANE), f32))
    return tuple(
        pl.pallas_call(
            functools.partial(attend_kernel, first, last, wide),
            out_shape=(
                jax.ShapeDtypeStruct((n, wide), bf16),
                jax.ShapeDtypeStruct((heads, n), f32),
            ),
            compiler_params=pltpu.CompilerParams(vmem_limit_bytes=28 * 1024 * 1024),
            cost_estimate=COST,
        )(qkv, qf, kf, *old)
    )


def back_kernel(first, last, wide, qkv_ref, do_ref, qf_ref, kf_ref, lse_ref, old_ref, out_ref):
    n = qkv_ref.shape[0]
    scale = HD ** -0.5
    scale_two = scale * 1.4426950408889634
    zero = jnp.zeros((), bf16)
    if first == 0:
        out_ref[...] = jnp.zeros_like(out_ref)
    else:
        out_ref[...] = old_ref[...]

    def head(h, carry):
        start, off = window(h, wide)
        inside, feature = lane_masks(off, n)
        at = pl.ds(start, WIN)
        at_k, at_v = pl.ds(start + wide, WIN), pl.ds(start + 2 * wide, WIN)
        k_win = qkv_ref[:, at_k]
        k = jnp.where(inside, k_win, jnp.where(feature, kf_ref[...], zero))
        k_t = jnp.where(inside, k_win, zero).T
        v = qkv_ref[:, at_v]
        dk, dv = None, None
        for i in range(n // CHUNK):
            rows = slice(i * CHUNK, (i + 1) * CHUNK)
            q_win = qkv_ref[rows, at]
            q = jnp.where(feature[:CHUNK], qf_ref[rows, :], q_win)
            q_only = jnp.where(inside[:CHUNK], q_win, zero)
            do = jnp.where(inside[:CHUNK], do_ref[rows, at], zero)
            s = lax.dot_general(k, q, NT, preferred_element_type=f32)
            p = jnp.exp2(s * scale_two - lse_ref[pl.ds(h, 1), rows])
            dp = lax.dot_general(v, do, NT, preferred_element_type=f32)
            part = lax.dot_general(p.astype(bf16), do, NN, preferred_element_type=f32)
            dv = part if dv is None else dv + part
            inner = jnp.sum(p * dp, axis=0, keepdims=True)
            ds = (p * (dp - inner)).astype(bf16)
            part = lax.dot_general(ds, q_only, NN, preferred_element_type=f32)
            dk = part if dk is None else dk + part
            dq = lax.dot_general(k_t, ds, NN, preferred_element_type=f32).T
            dq = (dq * scale).astype(bf16)
            out_ref[rows, at] = jnp.where(inside[:CHUNK], dq, out_ref[rows, at])
        out_ref[:, at_k] = jnp.where(inside, (dk * scale).astype(bf16), out_ref[:, at_k])
        out_ref[:, at_v] = jnp.where(inside, dv.astype(bf16), out_ref[:, at_v])
        return carry

    lax.fori_loop(first, last, head, 0)


def attend_back(first, last, qkv, do, qf, kf, lse, *old):
    n, wide = qkv.shape[0], qkv.shape[1] // 3
    if not old:
        old = (jnp.zeros((16, LANE), bf16),)
    return pl.pallas_call(
        functools.partial(back_kernel, first, last, wide),
        out_shape=jax.ShapeDtypeStruct(qkv.shape, bf16),
        compiler_params=pltpu.CompilerParams(vmem_limit_bytes=36 * 1024 * 1024),
        cost_estimate=COST,
    )(qkv, do, qf, kf, lse, *old)


def norm_parts(values):
    center = jnp.mean(values, axis=-1, keepdims=True)
    centered = values - center
    spread = jnp.mean(centered * centered, axis=-1, keepdims=True)
    inverse = lax.rsqrt(spread + norm_epsilon)
    return centered * inverse, inverse


def out_norm_kernel(
    core_ref, x_ref, a_ref, b_ref, w_ref, v_ref, bias_ref, gain_ref, shift_ref, res_ref, norm_ref
):
    half, cut = a_ref.shape[1], w_ref.shape[1]
    width = x_ref.shape[1]
    a, b = a_ref[...], b_ref[...]
    mine = dot(a, w_ref[:half, :]) + dot(b, w_ref[half:, :])
    theirs = dot(a, v_ref[half:, :]) + dot(b, v_ref[:half, :])
    first = core_ref[0] == 0

    @pl.when(first)
    def _():
        res_ref[:, :cut] = mine
        res_ref[:, cut:] = theirs[:, : width - cut]

    @pl.when(jnp.logical_not(first))
    def _():
        res_ref[:, :cut] = theirs
        res_ref[:, cut:] = mine[:, : width - cut]

    values = res_ref[...] + x_ref[...].astype(f32) + bias_ref[...]
    res_ref[...] = values
    unit, _ = norm_parts(values)
    norm_ref[...] = (unit * gain_ref[...] + shift_ref[...]).astype(bf16)


def out_norm(core, x, a, b, w, v, bias, gain, shift):
    t, width = x.shape
    tile = 128
    rows = lambda cols: pl.BlockSpec((tile, cols), lambda i: (i, 0))
    all_of = lambda v: pl.BlockSpec(v.shape, lambda i: (0, 0))
    return tuple(
        pl.pallas_call(
            out_norm_kernel,
            grid=(t // tile,),
            out_shape=[
                jax.ShapeDtypeStruct((t, width), f32),
                jax.ShapeDtypeStruct((t, width), bf16),
            ],
            in_specs=[
                pl.BlockSpec(memory_space=pltpu.SMEM),
                rows(width), rows(a.shape[1]), rows(b.shape[1]), all_of(w), all_of(v),
                all_of(bias), all_of(gain), all_of(shift),
            ],
            out_specs=[rows(width), rows(width)],
            compiler_params=pltpu.CompilerParams(vmem_limit_bytes=16 * 1024 * 1024),
            cost_estimate=COST,
        )(core, x, a, b, w, v, bias, gain, shift)
    )


def norm_back_kernel(t_ref, came_ref, pass_ref, values_ref, gain_ref, out_ref, low_ref, sum_ref):
    t = t_ref[...] + came_ref[...].astype(f32)
    unit, inverse = norm_parts(values_ref[...].astype(f32))
    scaled = t * gain_ref[...]
    along = jnp.mean(scaled * unit, axis=-1, keepdims=True)
    grad = (scaled - jnp.mean(scaled, axis=-1, keepdims=True) - unit * along) * inverse
    grad = pass_ref[...].astype(f32) + grad
    out_ref[...] = grad
    low = grad.astype(bf16)
    low_ref[...] = low

    @pl.when(pl.program_id(0) == 0)
    def _():
        sum_ref[...] = jnp.zeros_like(sum_ref)

    sum_ref[0:1, :] += jnp.sum(t * unit, axis=0, keepdims=True)
    sum_ref[1:2, :] += jnp.sum(t, axis=0, keepdims=True)
    sum_ref[2:3, :] += jnp.sum(low.astype(f32), axis=0, keepdims=True)


def norm_back(t, came, passed, values, gain):
    n, width = t.shape
    tile = 128
    rows = pl.BlockSpec((tile, width), lambda i: (i, 0))
    return tuple(
        pl.pallas_call(
            norm_back_kernel,
            grid=(n // tile,),
            out_shape=[
                jax.ShapeDtypeStruct((n, width), f32),
                jax.ShapeDtypeStruct((n, width), bf16),
                jax.ShapeDtypeStruct((8, width), f32),
            ],
            in_specs=[rows] * 4 + [pl.BlockSpec((1, width), lambda i: (0, 0))],
            out_specs=[rows, rows, pl.BlockSpec((8, width), lambda i: (0, 0))],
            compiler_params=pltpu.CompilerParams(vmem_limit_bytes=16 * 1024 * 1024),
            cost_estimate=COST,
        )(t, came, passed, values, gain)
    )


def column_sum(rows):
    return jnp.sum(rows.astype(f32), axis=0)


def gelu_and_slope(z):
    root = 0.7978845608028654
    cube = 0.044715 * root
    square = z * z
    h = 0.5 + 0.5 * jnp.tanh(z * (root + cube * square))
    value = z * h
    return value, h + 2.0 * value * (1.0 - h) * (root + 3.0 * cube * square)


def up_kernel(n_ref, w_ref, b_ref, value_ref, slope_ref):
    cols = w_ref.shape[1]
    step = 512
    for left in range(0, cols, step):
        part = slice(left, min(left + step, cols))
        value, slope = gelu_and_slope(dot(n_ref[...], w_ref[:, part]) + b_ref[:, part])
        value_ref[:, part] = value.astype(bf16)
        slope_ref[:, part] = slope.astype(bf16)


def hidden_kernel(g_ref, w_ref, s_ref, out_ref, sum_ref):
    cols = w_ref.shape[1]
    step = 512

    @pl.when(pl.program_id(0) == 0)
    def _():
        sum_ref[...] = jnp.zeros_like(sum_ref)

    for left in range(0, cols, step):
        part = slice(left, min(left + step, cols))
        out = (dot(g_ref[...], w_ref[:, part]) * s_ref[:, part].astype(f32)).astype(bf16)
        out_ref[:, part] = out
        sum_ref[0:1, part] += jnp.sum(out.astype(f32), axis=0, keepdims=True)


def hidden_back(g, w, s):
    t, width = g.shape
    cols = w.shape[1]
    tile = 256
    row = pl.BlockSpec((tile, cols), lambda i: (i, 0))
    return tuple(
        pl.pallas_call(
            hidden_kernel,
            grid=(t // tile,),
            out_shape=[
                jax.ShapeDtypeStruct((t, cols), bf16),
                jax.ShapeDtypeStruct((8, cols), f32),
            ],
            in_specs=[
                pl.BlockSpec((tile, width), lambda i: (i, 0)),
                pl.BlockSpec(w.shape, lambda i: (0, 0)),
                row,
            ],
            out_specs=[row, pl.BlockSpec((8, cols), lambda i: (0, 0))],
            compiler_params=pltpu.CompilerParams(vmem_limit_bytes=28 * 1024 * 1024),
            cost_estimate=COST,
        )(g, w, s)
    )


def up_gelu(n, w, b):
    t, width = n.shape
    cols = w.shape[1]
    tile = 256
    out = pl.BlockSpec((tile, cols), lambda i: (i, 0))
    return tuple(
        pl.pallas_call(
            up_kernel,
            grid=(t // tile,),
            out_shape=[jax.ShapeDtypeStruct((t, cols), bf16)] * 2,
            in_specs=[
                pl.BlockSpec((tile, width), lambda i: (i, 0)),
                pl.BlockSpec(w.shape, lambda i: (0, 0)),
                pl.BlockSpec(b.shape, lambda i: (0, 0)),
            ],
            out_specs=[out, out],
            compiler_params=pltpu.CompilerParams(vmem_limit_bytes=28 * 1024 * 1024),
            cost_estimate=COST,
        )(n, w, b)
    )


def on_device(
    tokens,
    lengths,
    norm1_gain,
    norm1_bias,
    w_query,
    query_bias,
    w_key,
    w_value,
    value_bias,
    w_out,
    out_bias,
    norm2_gain,
    norm2_bias,
    w_up,
    up_bias,
    w_down,
    down_bias,
    cotangent,
):
    at = Places(lax.axis_size("rows"), lax.axis_size("seq"))
    line = Line()
    micro, rows_here, local_len, width = tokens.shape
    full_len = local_len * lax.axis_size("seq")
    own = 2 * rows_here * local_len
    own_rows, hidden_width = w_up.shape
    at.own_rows = own_rows
    chip_rows = 2 * own_rows
    zero_core = at.c == 0
    nz = at.nz
    head_width = width // 2
    wide = -(-head_width // LANE) * LANE
    out_cut = wide
    half_width = -(-hidden_width // (2 * LANE)) * LANE

    def by_core(a, b):
        return jnp.where(zero_core, a, b)

    def swapped_in(mine, came):
        low = jnp.where(at.x == 0, mine, came)
        high = jnp.where(at.x == 0, came, mine)
        return jnp.stack([low, high]).reshape(own, width)

    def for_swap_out(values):
        values = values.reshape(2, rows_here, local_len, width)
        return pick(values, at.x), pick(values, 1 - at.x).astype(bf16)

    def swapped_out(mine, came):
        came = came.astype(mine.dtype)
        return jnp.stack([jnp.where(at.x == 0, mine, came), jnp.where(at.x == 0, came, mine)])

    def fill(v, to):
        return jnp.pad(v, ((0, 0), (0, to - v.shape[1])))

    vectors = jnp.stack(
        [norm1_gain, norm1_bias, query_bias, value_bias, out_bias, norm2_gain, norm2_bias, down_bias]
    )
    vectors = dot(jnp.eye(own_rows, dtype=bf16), vectors, NT, bf16)
    me = lax.axis_index("rows") * lax.axis_size("seq") + lax.axis_index("seq")

    spot = jnp.arange(chip_rows, dtype=jnp.int32)
    spot = flip(at.c, spot // own_rows) * own_rows + spot % own_rows
    turn = (jnp.arange(chip_rows, dtype=jnp.int32)[:, None] == spot[None, :]).astype(bf16)
    s_cut, u_cut, d_cut = 10 * LANE, 13 * LANE, 10 * LANE
    s_wide, u_wide, d_wide = 3 * wide, out_cut + half_width, half_width
    s_pieces = Pieces(at, chip_rows, s_wide)
    u_pieces = Pieces(at, chip_rows, u_wide)
    d_pieces = Pieces(at, chip_rows, d_wide)

    def qkv_half(c):
        part = slice(c * head_width, (c + 1) * head_width)
        query = fill(jnp.concatenate([w_query[:, part], vectors], axis=1), wide)
        return jnp.concatenate([query] + [fill(w[:, part], wide) for w in (w_key, w_value)], axis=1)

    def chip_shard(turn, keep, came):
        return dot(turn, jnp.concatenate([keep, came], axis=0), NN, bf16)

    def pair_parts(cut):
        def step(mine, low, high):
            pair = jnp.stack([mine, jnp.concatenate([low, high], axis=1)])
            return pair, pair[:, :, :cut], pair[:, :, cut:]

        return step

    def stack_parts(cut):
        def step(*v):
            return jnp.stack([p[..., :cut] for p in v]), jnp.stack([p[..., cut:] for p in v])

        return step

    def add_pair(pieces, k, array, cut):
        cols = pieces.cols
        pieces.add(
            array,
            [((a,), 0, (k, a, 0), 0, cut) for a in range(2)]
            + [((a,), cut, (k, 0, a), cut, cols - cut) for a in range(2)],
        )

    def add_across(pieces, ks, low, high, cut):
        cols = pieces.cols
        index = lambda i, a: (a,) if len(ks) == 1 and low.ndim == 3 else (i, a)
        every = [(i, k, a) for i, k in enumerate(ks) for a in range(2)]
        pieces.add(low, [(index(i, a), 0, (k, a, 1), 0, cut) for i, k, a in every])
        pieces.add(high, [(index(i, a), 0, (k, 1, a), cut, cols - cut) for i, k, a in every])

    def add_line(pieces, k, array, dx, dy):
        pieces.add(array, [((), 0, (k, dx, dy), 0, pieces.cols)])

    low, high = qkv_half(0), qkv_half(1)
    keep_s, give_s = by_core(low, high), by_core(high, low)
    core = line.start(give_s, at.to_core)
    up_full = fill(w_up, 2 * half_width)
    down_full = fill(dot(jnp.eye(own_rows, dtype=bf16), w_down, NT, bf16), 2 * half_width)
    low = [w_out[:, :out_cut], up_full[:, :half_width], down_full[:, :half_width]]
    high = [fill(w_out[:, out_cut:], out_cut), up_full[:, half_width:], down_full[:, half_width:]]
    low, high = jnp.concatenate(low, axis=1), jnp.concatenate(high, axis=1)
    keep_f, give_f = by_core(low, high), by_core(high, low)

    def other_shards(turn, keep, came):
        both = jnp.concatenate([keep, came], axis=0)
        u, d = dot(turn, both[:, :u_wide], NN, bf16), dot(turn, both[:, u_wide:], NN, bf16)
        return u, u[:, :u_cut], u[:, u_cut:], d, d[:, :d_cut], d[:, d_cut:]

    def tokens_step(tokens, came):
        return swapped_in(pick(tokens, at.x), came)

    def unit_step(own, other):
        return norm_parts(jnp.concatenate([own, other]).astype(f32))[0]

    def stack(*v):
        return jnp.stack(v)

    def low_of(*v):
        return jnp.concatenate([p[..., :s_cut] for p in v])

    def high_of(*v):
        return jnp.concatenate([p[..., s_cut:] for p in v])

    half_z = nz // 2
    ring = [line.run(chip_shard, turn, keep_s, line.done(core))]
    z, y = line.start(ring[0], at.to_z), line.start(ring[0], at.to_y)
    x = line.start(line.run(lambda v: pick(v, 1 - at.x), tokens), at.to_x)
    core = line.start(give_f, at.to_core)
    ring.append(line.done(z))
    z = line.start(ring[-1], at.to_z)
    y_zero, tokens_came, core = line.done(y, x, core)
    shard_u, u_low, u_high, shard_d, d_low, d_high = line.run(other_shards, turn, keep_f, core)
    tokens_own = line.run(tokens_step, tokens, tokens_came)
    for _ in range(2, nz):
        ring.append(line.done(z))
        if len(ring) < nz:
            z = line.start(ring[-1], at.to_z)
        if len(ring) == 3:
            x, y = line.start(u_low, at.to_x), line.start(u_high, at.to_y)
            core = line.start(tokens_own, at.to_core)
    u_low, u_high, ring_tokens = line.done(x, y, core)
    u_pair, u_low, u_high = line.run(pair_parts(u_cut), shard_u, u_low, u_high)
    x = line.start(line.run(stack, *ring[:half_z]), at.to_x)
    y = line.start(line.run(stack, *ring[1:]), at.to_y)
    u_ring = [u_pair]
    z = line.start(u_pair, at.to_z)
    later = line.run(stack, *ring[half_z:])
    xs = [line.done(x)]
    x = line.start(later, at.to_x)
    ys = [y_zero, line.done(y)]
    y = line.start(line.run(low_of, xs[0]), at.to_y)
    x_both = line.start(line.run(high_of, ys[0][None], ys[1]), at.to_x)
    u_ring.append(line.done(z))
    xs.append(line.done(x))
    y_later = line.start(line.run(low_of, xs[1]), at.to_y)
    unit_one = line.run(unit_step, tokens_own, ring_tokens)
    z = line.start(u_ring[-1], at.to_z)
    both_y = [line.done(y)]
    both_x = line.done(x_both)
    both_y.append(line.done(y_later))

    row_lengths = pick(lengths, at.x)[0]
    ends_at = jnp.cumsum(row_lengths)
    inside = jnp.arange(own, dtype=jnp.int32)

    def segment_of(core):
        spots = (inside // local_len) * (full_len // 2) + core * local_len + inside % local_len
        return jnp.sum((spots[:, None] >= ends_at[None, :]).astype(jnp.int32), axis=-1)

    segments = jnp.concatenate([segment_of(at.c), segment_of(1 - at.c)])
    lane = (jnp.arange(WIN, dtype=jnp.int32) % 4)[None, :]
    feat_q = (segments[:, None] == lane).astype(bf16)
    feat_k = jnp.where(segments[:, None] == lane, 0.0, -BIG).astype(bf16)
    feat_q, feat_k = line.run(lambda *v: v, feat_q, feat_k)
    for k in range(nz):
        add_line(s_pieces, k, ring[k], 0, 0)
    for i, ks in enumerate((range(half_z), range(half_z, nz))):
        s_pieces.add(xs[i], [((j,), 0, (k, 1, 0), 0, s_wide) for j, k in enumerate(ks)])
        s_pieces.add(both_y[i], [((j,), 0, (k, 1, 1), 0, s_cut) for j, k in enumerate(ks)])
    add_line(s_pieces, 0, ys[0], 0, 1)
    s_pieces.add(ys[1], [((k - 1,), 0, (k, 0, 1), 0, s_wide) for k in range(1, nz)])
    s_pieces.add(both_x, [((k,), 0, (k, 1, 1), s_cut, s_wide - s_cut) for k in range(nz)])

    weight_s = s_pieces.place(line, (s_wide,))
    chosen = jnp.eye(vectors.shape[1], s_wide, head_width, dtype=bf16)
    left = (head_width // LANE) * LANE
    vectors = line.run(
        lambda e, w: dot(e[:, left:wide], w[:, left:wide], NT), chosen, weight_s
    )
    gain_one, shift_one, bias_q, bias_v, bias_o, gain_two, shift_two, bias_d = [
        vectors[i][None] for i in range(8)
    ]
    halves = [by_core(b[:, :head_width], b[:, head_width:]) for b in (bias_q, bias_v)]
    bias_qkv = jnp.concatenate(
        [fill(halves[0], wide), jnp.zeros((1, wide), f32), fill(halves[1], wide)], axis=1
    )
    normed = line.run(lambda u, g, s: (u * g + s).astype(bf16), unit_one, gain_one, shift_one)
    u_ring.append(line.done(z))
    for _ in range(3, nz - 1):
        u_ring.append(line.done(line.start(u_ring[-1], at.to_z)))
    x_pair, y_pair = line.start(d_low, at.to_x), line.start(d_high, at.to_y)
    x, y = line.start(u_high, at.to_x), line.start(u_low, at.to_y)
    z = line.start(u_ring[-1], at.to_z)
    qkv = line.run(lambda n, w, b: (dot(n, w) + b).astype(bf16), normed, weight_s, bias_qkv)
    add_pair(u_pieces, 0, u_pair, u_cut)
    d_low, d_high = line.done(x_pair, y_pair)
    d_pair, d_low, d_high = line.run(pair_parts(d_cut), shard_d, d_low, d_high)
    high, low = line.done(x, y)
    add_across(u_pieces, [0], low, high, u_cut)
    low, high = line.run(stack_parts(u_cut), *u_ring[1:half_z])
    x, y = line.start(high, at.to_x), line.start(low, at.to_y)
    heads = H // 2
    attended, lse = line.run(functools.partial(attend, 0, heads // 2), qkv, feat_q, feat_k)
    u_ring.append(line.done(z))
    high, low = line.done(x, y)
    add_across(u_pieces, list(range(1, half_z)), low, high, u_cut)
    low, high = line.run(stack_parts(u_cut), *u_ring[half_z:-1])
    z = line.start(d_pair, at.to_z)
    x, y = line.start(high, at.to_x), line.start(low, at.to_y)
    low, high = line.run(stack_parts(u_cut), u_ring[-1])
    attended, lse = line.run(
        functools.partial(attend, heads // 2, heads), qkv, feat_q, feat_k, attended, lse
    )
    d_ring = [d_pair, line.done(z)]
    for k in range(1, nz):
        add_pair(u_pieces, k, u_ring[k], u_cut)
    high_two, low_two = line.done(x, y)
    add_across(u_pieces, list(range(half_z, nz - 1)), low_two, high_two, u_cut)
    attended_own, give = line.run(
        lambda a: (a[:own, :head_width], a[own:, :head_width]), attended
    )
    core = line.start(give, at.to_core)
    x, y = line.start(high, at.to_x), line.start(low, at.to_y)
    z = line.start(d_ring[-1], at.to_z)
    cotangent_theirs = line.run(lambda v: pick(v, 1 - at.x), cotangent)
    attended_other = line.done(core)
    high, low = line.done(x, y)
    add_across(u_pieces, [nz - 1], low, high, u_cut)
    x, y = line.start(cotangent_theirs, at.to_x), line.start(d_low, at.to_y)
    weight_half_o, weight_u = u_pieces.place(line, (out_cut, half_width), (True, False))
    d_ring.append(line.done(z))
    out_came, d_low = line.done(x, y)
    core = line.start(weight_half_o, at.to_core)
    for _ in range(3, nz - 1):
        d_ring.append(line.done(line.start(d_ring[-1], at.to_z)))
    x = line.start(d_high, at.to_x)
    low, high = line.run(stack_parts(d_cut), *d_ring[1:])
    y = line.start(low, at.to_y)
    z = line.start(d_ring[-1], at.to_z)
    grad_out = line.run(
        lambda v, came: swapped_in(pick(v, at.x), came), cotangent, out_came
    )
    other_half_o = line.done(core)
    zero_flag = jnp.reshape(at.c, (1,)).astype(jnp.int32)
    residual_one, normed_two_own = line.run(
        out_norm, zero_flag, tokens_own, attended_own, attended_other, weight_half_o, other_half_o,
        bias_o, gain_two, shift_two,
    )
    add_pair(d_pieces, 0, d_pair, d_cut)
    d_high = line.done(x)
    add_across(d_pieces, [0], d_low, d_high, d_cut)
    low = line.done(y)
    d_ring.append(line.done(z))
    core = line.start(normed_two_own, at.to_core)
    x = line.start(high, at.to_x)
    low_last, high_last = line.run(stack_parts(d_cut), d_ring[-1])
    y, x_last = line.start(low_last, at.to_y), line.start(high_last, at.to_x)
    normed_two = line.run(
        lambda a, b: jnp.concatenate([a, b]), normed_two_own, line.done(core)
    )
    bias_up = fill(up_bias.astype(f32)[None], 2 * half_width)
    bias_up = by_core(bias_up[:, :half_width], bias_up[:, half_width:])

    def up_step(n, w, b):
        return up_gelu(n, w, b)

    active, slope = line.run(up_step, normed_two, weight_u, bias_up)
    high = line.done(x)
    add_across(d_pieces, list(range(1, nz - 1)), low, high, d_cut)
    low, high = line.done(y, x_last)
    add_across(d_pieces, [nz - 1], low, high, d_cut)
    for k in range(1, nz):
        add_pair(d_pieces, k, d_ring[k], d_cut)
    core = line.start(grad_out, at.to_core)
    weight_d = d_pieces.place(line, (half_width,))
    grad_out_all = line.run(lambda a, b: jnp.concatenate([a, b]), grad_out, line.done(core))

    d_down = line.run(lambda g, a: dot(g, a, TN, bf16), grad_out_all, active)
    quarter = nz // 4
    d_scatter = Scatter(line, at, d_cut, True, (quarter, 2 * quarter, 3 * quarter))
    d_scatter.cut_out(d_down)
    d_scatter.begin()
    grad_hidden, hidden_sums = line.run(hidden_back, grad_out_all, weight_d, slope)
    d_scatter.arrive()
    hidden_sums = hidden_sums[0]

    def rows_other(a, w):
        return dot(a[own:], w, NT, bf16)

    def rows_own(a, w):
        return dot(a[:own], w, NT)

    d_scatter.begin()
    give = line.run(rows_other, grad_hidden, weight_u)
    back_own = line.run(rows_own, grad_hidden, weight_u)
    d_scatter.arrive()
    core = line.start(give, at.to_core)
    d_scatter.begin()
    d_up = line.run(lambda n, g: dot(n, g, TN, bf16), normed_two, grad_hidden)
    core = line.done(core)
    d_scatter.arrive()
    d_scatter.begin()
    grad_residual, grad_branch, sums_two = line.run(
        norm_back, back_own, core, grad_out, residual_one, gain_two
    )

    def branch_columns(g):
        a, b = g[:, :out_cut], fill(g[:, out_cut:], out_cut)
        return by_core(a, b), by_core(b, a)

    branch_own, branch_peer = line.run(branch_columns, grad_branch)

    def heads_back(a, v, b, w):
        return (dot(a, v, NT) + dot(b, w, NT)).astype(bf16)

    def out_weight(a, b, g):
        return jnp.concatenate([dot(a, g, TN, bf16), dot(b, g, TN, bf16)])

    give = line.run(
        heads_back, branch_own, weight_half_o[head_width:], branch_peer, other_half_o[:head_width]
    )
    d_out_peer = line.run(out_weight, attended_other, attended_own, branch_peer)
    d_scatter.arrive()
    core = line.start(give, at.to_core)
    d_out_came = line.start(d_out_peer, at.to_core)
    d_scatter.keep()
    u_scatter = Scatter(line, at, u_cut, True, (nz // 2,))
    u_scatter.cut_out(d_up)
    u_scatter.begin()
    grad_att_own = line.run(
        heads_back, branch_own, weight_half_o[:head_width], branch_peer, other_half_o[head_width:]
    )
    grad_att = line.run(
        lambda a, b: fill(jnp.concatenate([a, b]), wide), grad_att_own, line.done(core)
    )

    def out_weight_own(a, b, g, came):
        total = jnp.concatenate([dot(a, g, TN), dot(b, g, TN)]) + came.astype(f32)
        half = total.shape[0] // 2
        low, high = total[:half], total[half:]
        return jnp.concatenate([by_core(low, high), by_core(high, low)]).astype(bf16)

    d_out = line.run(
        out_weight_own, attended_own, attended_other, branch_own, line.done(d_out_came)
    )
    d_scatter.arrive()
    u_scatter.arrive()
    d_scatter.ring()
    u_scatter.begin()
    u_scatter.more(d_out)
    d_qkv = line.run(
        functools.partial(attend_back, 0, heads // 2), qkv, grad_att, feat_q, feat_k, lse
    )
    d_scatter.arrive()
    u_scatter.arrive()
    d_scatter.ring()
    u_scatter.keep()
    d_qkv = line.run(
        functools.partial(attend_back, heads // 2, heads), qkv, grad_att, feat_q, feat_k, lse, d_qkv
    )
    d_scatter.arrive()
    d_scatter.last_start()
    s_scatter = Scatter(line, at, 8 * LANE, False)
    d_s = line.run(lambda n, g: dot(n, g, TN, bf16), normed, d_qkv)
    give = line.run(rows_other, d_qkv, weight_s)
    core = line.start(give, at.to_core)
    s_scatter.cut_out(d_s)
    s_scatter.begin()
    u_scatter.ring()
    back_own = line.run(rows_own, d_qkv, weight_s)
    d_scatter.last()
    grad_tokens, _, sums_one = line.run(
        norm_back, back_own, line.done(core), grad_residual, tokens_own, gain_one
    )
    token_mine, token_theirs = line.run(for_swap_out, grad_tokens)
    give = line.run(rows_other, active, weight_d)
    result_own = line.run(rows_own, active, weight_d)
    s_scatter.arrive()
    u_scatter.arrive()
    def full(half):
        zeros = jnp.zeros_like(half)
        return jnp.concatenate([by_core(half, zeros), by_core(zeros, half)])

    qkv_sums = column_sum(d_qkv)
    sums = jnp.concatenate(
        [
            column_sum(grad_out),
            sums_two[2],
            sums_two[0],
            sums_two[1],
            full(qkv_sums[:head_width]),
            full(qkv_sums[2 * wide : 2 * wide + head_width]),
            sums_one[0],
            sums_one[1],
            full(hidden_sums),
        ]
    )
    sums = jnp.pad(sums, (0, -sums.shape[0] % (8 * LANE))).reshape(-1, LANE)
    sums = line.run(lambda v: v, sums)
    core = line.start(give, at.to_core)
    sums_at = Sums(line, at, sums)
    sums_at.step()
    s_scatter.keep()
    u_scatter.ring()
    block_output = line.run(
        lambda r, t, c, b: (r + t + c.astype(f32) + b).astype(bf16),
        residual_one, result_own, line.done(core), bias_d,
    )
    out_mine, out_theirs = line.run(for_swap_out, block_output)
    s_scatter.arrive()
    sums_at.step()
    s_scatter.second()
    token_came = line.start(token_theirs, at.to_x)
    u_scatter.arrive()
    sums_at.step()
    u_scatter.last_start()
    s_scatter.ring()
    out_came = line.start(out_theirs, at.to_x)
    sums_at.step()
    s_scatter.ring()
    u_scatter.last()
    sums_at.step()
    s_scatter.last()
    sums_at.step()
    sums = sums_at.result()
    grad_tokens = swapped_out(token_mine, line.done(token_came))
    block_output = swapped_out(out_mine, line.done(out_came))
    sums = sums.reshape(-1)

    def my_part(i):
        return lax.dynamic_slice_in_dim(sums, i * width + me * own_rows, own_rows)

    def joined(parts, left, right):
        return jnp.concatenate([p[:, left:right] for p in parts], axis=1)

    d_down, d_up, d_qkv = d_scatter.result(), u_scatter.result(), s_scatter.result()
    return (
        block_output,
        grad_tokens,
        my_part(6),
        my_part(7),
        joined(d_qkv, 0, head_width),
        my_part(4),
        joined(d_qkv, wide, wide + head_width),
        joined(d_qkv, 2 * wide, 2 * wide + head_width),
        my_part(5),
        joined(d_up, half_width, u_wide)[:, :width],
        my_part(1),
        my_part(2),
        my_part(3),
        joined(d_up, 0, half_width)[:, :hidden_width],
        sums[8 * width : 8 * width + hidden_width],
        joined(d_down, 0, half_width)[:, :hidden_width].T,
        my_part(0),
    )


def solution(mesh):
    feature = P(AXES)
    matrix = P(AXES, None)
    row = P(None, "rows", "seq", None)
    return jax.shard_map(
        on_device,
        mesh=mesh,
        in_specs=(
            row,
            P(None, "rows", None),
            feature,
            feature,
            matrix,
            feature,
            matrix,
            matrix,
            feature,
            matrix,
            feature,
            feature,
            feature,
            matrix,
            P(),
            P(None, AXES),
            feature,
            row,
        ),
        out_specs=(
            row,
            row,
            feature,
            feature,
            matrix,
            feature,
            matrix,
            matrix,
            feature,
            matrix,
            feature,
            feature,
            feature,
            matrix,
            P(),
            P(None, AXES),
            feature,
        ),
        check_vma=False,
    )
```

```python
import functools

import jax
import jax.numpy as jnp
from jax import lax
from jax.experimental import pallas as pl
from jax.experimental.pallas import tpu as pltpu
from jax.sharding import PartitionSpec as P

H = 16
HD = 72
AXES = ("rows", "seq")
norm_epsilon = 1e-06
BIG = 1e30
LANE = 128
WIN = 256
bf16 = jnp.bfloat16
f32 = jnp.float32
COST = pl.CostEstimate(flops=5 * 10**9, bytes_accessed=10**7, transcendentals=10**6)
NT = (((1,), (1,)), ((), ()))
TN = (((0,), (0,)), ((), ()))
NN = (((1,), (0,)), ((), ()))


def dot(a, b, dims=NN, out=f32):
    return lax.dot_general(a, b, dims, preferred_element_type=f32).astype(out)


class Places:
    def __init__(self, n_rows, n_seq):
        self.nz, self.ny, self.nx, self.nc = n_rows // 2, 2, n_seq // 2, 2
        every = [
            (z, y, x, c)
            for z in range(self.nz)
            for y in range(2)
            for x in range(2)
            for c in range(2)
        ]
        nz = self.nz

        def flat(z, y, x, c):
            return ((z * 2 + y) * 2 + x) * 2 + c

        def pairs(f):
            return [(flat(*t), flat(*f(*t))) for t in every]

        self.to_core = pairs(lambda z, y, x, c: (z, y, x, 1 - c))
        self.to_x = pairs(lambda z, y, x, c: (z, y, 1 - x, c))
        self.to_y = pairs(lambda z, y, x, c: (z, 1 - y, x, c))
        self.to_z = pairs(lambda z, y, x, c: ((z + 1) % nz, y, x, c))
        assert nz & (nz - 1) == 0
        self.z_swaps = [
            pairs(lambda z, y, x, c, bit=1 << i: (z ^ bit, y, x, c))
            for i in range(nz.bit_length() - 1)
        ]
        r, s = lax.axis_index("rows"), lax.axis_index("seq")
        self.z, self.y, self.x, self.c = r // 2, r % 2, s // 2, s % 2


def send(value, pairs):
    return lax.ppermute(value, AXES, pairs)


class Going:
    def __init__(self, value):
        self.value, self.here = value, False


class Line:
    def __init__(self):
        self.token = jnp.zeros((8, LANE), f32)
        self.queue = []

    def pin(self, *values):
        return lax.optimization_barrier((values, self.token))[0]

    def close(self, *values):
        values, self.token = lax.optimization_barrier((values, self.token))
        return values if len(values) > 1 else values[0]

    def done(self, *going):
        while not all(g.here for g in going):
            first = self.queue.pop(0)
            first.value, first.here = self.close(first.value), True
        return [g.value for g in going] if len(going) > 1 else going[0].value

    def run(self, step, *values):
        out = step(*self.pin(*values))
        return self.close(*out) if isinstance(out, tuple) else self.close(out)

    def start(self, value, pairs):
        self.queue.append(Going(send(self.pin(value)[0], pairs)))
        return self.queue[-1]


def flip(here, by):
    return here + by - 2 * by * here


def place_kernel(n_in, n_out, plan, *refs):
    dyn = refs[0]
    ins, outs, sem = refs[1 : 1 + n_in], refs[1 + n_in : 1 + n_in + n_out], refs[1 + n_in + n_out]
    nz = outs[0].shape[0]
    copies = []
    for j, (i, src, src_col, out, dst, dst_col, wide) in enumerate(plan):
        zi, yi, xi = dst(dyn[0], dyn[1], dyn[2])
        zi = lax.rem(zi + dyn[3 + out], nz)
        source = ins[i].at[(*src, slice(None), pl.ds(src_col, wide))]
        target = outs[out].at[zi, yi, xi, :, pl.ds(dst_col, wide)]
        copies.append(pltpu.make_async_copy(source, target, sem.at[j]))
    for copy in copies:
        copy.start()
    for copy in copies:
        copy.wait()


def place(at, ins, plan, rows, widths, turned):
    turns = [jnp.where(at.c == 1, at.nz // 2 if t else 0, 0) for t in turned]
    cut_plan = []
    for i, src, src_col, dst, col, wide in plan:
        left = 0
        for out, out_wide in enumerate(widths):
            low, high = max(col, left), min(col + wide, left + out_wide)
            if low < high:
                cut_plan.append((i, src, src_col + low - col, out, dst, low - left, high - low))
            left += out_wide
    shapes = [(at.nz, 2, 2, rows, w) for w in widths]
    if rows % 8 == 0:
        dyn = jnp.stack([at.z, at.y, at.x, *turns]).astype(jnp.int32)
        outs = pl.pallas_call(
            functools.partial(place_kernel, len(ins), len(widths), cut_plan),
            out_shape=[jax.ShapeDtypeStruct(shape, ins[0].dtype) for shape in shapes],
            in_specs=[pl.BlockSpec(memory_space=pltpu.SMEM)]
            + [pl.BlockSpec(memory_space=pl.ANY)] * len(ins),
            out_specs=[pl.BlockSpec(memory_space=pltpu.VMEM)] * len(widths),
            scratch_shapes=[pltpu.SemaphoreType.DMA((len(cut_plan),))],
            compiler_params=pltpu.CompilerParams(vmem_limit_bytes=16 * 1024 * 1024),
            cost_estimate=COST,
        )(dyn, *ins)
    else:
        outs = [jnp.zeros(shape, ins[0].dtype) for shape in shapes]
        for i, src, src_col, out, dst, dst_col, wide in cut_plan:
            piece = ins[i][src][:, src_col : src_col + wide]
            zi, yi, xi = dst(at.z, at.y, at.x)
            zi = (zi + turns[out]) % at.nz
            outs[out] = lax.dynamic_update_slice(
                outs[out], piece[None, None, None], (zi, yi, xi, 0, dst_col)
            )
    return tuple(o.reshape(at.nz * 4 * rows, w) for o, w in zip(outs, widths))


class Pieces:
    def __init__(self, at, rows, cols):
        self.at, self.rows, self.cols = at, rows, cols
        self.arrays, self.plan = [], []

    def add(self, array, places):
        i, nz = len(self.arrays), self.at.nz
        self.arrays.append(array)
        for index, src_col, (k, dx, dy), col, wide in places:

            def slot(z, y, x, k=k, dx=dx, dy=dy):
                return lax.rem(z - k + nz, nz), flip(y, dy), flip(x, dx)

            self.plan.append((i, index, src_col, slot, col, wide))

    def place(self, line, widths, turned=(False, False)):
        return line.run(
            lambda *v: place(self.at, v, self.plan, self.rows, widths, turned[: len(widths)]),
            *self.arrays,
        )


def pick(values, i, axis=0):
    return lax.dynamic_index_in_dim(values, i, axis, keepdims=False)


class Scatter:
    def __init__(self, line, at, cut, pairs, ends=()):
        self.line, self.at, self.cut, self.pairs = line, at, cut, pairs
        self.ends = ends
        self.ring_at = 0
        self.total = self.low = self.high = self.extra = self.extra_came = None

    def blocks(self, total):
        at = self.at
        return total.reshape(at.nz, 2, 2, 2 * at.own_rows, total.shape[1])

    def cut_out(self, total):
        at, cut = self.at, self.cut
        self.whole = total
        self.low, self.high = [], []

        def step(total):
            v = self.blocks(total)
            low, high = pick(v[..., :cut], 1 - at.y, 1), pick(v[..., cut:], 1 - at.x, 2)
            ends = [0, *self.ends, at.nz]
            return tuple(v[i:j] for v in (low, high) for i, j in zip(ends[:-1], ends[1:]))

        self.parts = list(self.line.run(step, total))

    def begin(self):
        n = len(self.ends) + 1
        i = len(self.low)
        self.low.append(self.line.start(self.parts[i], self.at.to_y))
        self.high.append(self.line.start(self.parts[n + i], self.at.to_x))

    def more(self, total):
        self.extra = total
        part = self.line.run(lambda v: pick(self.blocks(v), 1 - self.at.x, 2), total)
        self.extra_came = self.line.start(part, self.at.to_x)

    def first_of(self, kept):
        return kept, pick(kept, (self.at.z - 1 + self.at.nz) % self.at.nz)

    def arrive(self):
        for going in (self.total, self.low, self.high, self.extra_came):
            if isinstance(going, Going):
                self.line.done(going)
            elif isinstance(going, list):
                self.line.done(*going)

    def keep_run(self):
        at, cut = self.at, self.cut
        came = self.line.done(*self.low, *self.high)
        n = len(self.low)
        extra = () if self.extra is None else (self.extra, self.line.done(self.extra_came))

        def step(total, *came):
            low, high = jnp.concatenate(came[:n]), jnp.concatenate(came[n : 2 * n])
            v = self.blocks(total)
            low = pick(v[..., :cut], at.y, 1).astype(f32) + low.astype(f32)
            high = pick(v[..., cut:], at.x, 2).astype(f32) + high.astype(f32)
            parts = [low, high]
            if extra:
                mine, other = came[2 * n :]
                parts.append(pick(self.blocks(mine), at.x, 2).astype(f32) + other.astype(f32))
            parts = [p.astype(bf16) for p in parts]
            if self.pairs:
                return self.first_of(jnp.concatenate(parts, axis=-1))
            low, high = parts
            return (
                pick(low, at.x, 1), pick(high, at.y, 1),
                pick(low, 1 - at.x, 1), pick(high, 1 - at.y, 1),
            )

        self.kept = self.line.run(step, self.whole, *came, *extra)
        self.whole = self.extra = self.extra_came = self.low = self.high = None

    def keep_start(self):
        kept = self.kept
        if self.pairs:
            self.kept = kept[0]
            self.total = self.line.start(kept[1], self.at.to_z)
        else:
            self.kept = kept[:2]
            self.low = self.line.start(kept[2], self.at.to_x)
            self.high = self.line.start(kept[3], self.at.to_y)

    def keep(self):
        self.keep_run()
        self.keep_start()

    def second(self):
        low, high = self.line.done(self.low, self.high)

        def step(kept_low, kept_high, low, high):
            low = (kept_low.astype(f32) + low.astype(f32)).astype(bf16)
            high = (kept_high.astype(f32) + high.astype(f32)).astype(bf16)
            return self.first_of(jnp.concatenate([low, high], axis=-1))

        self.kept, first = self.line.run(step, *self.kept, low, high)
        self.total = self.line.start(first, self.at.to_z)

    def ring(self):
        at, cut, k = self.at, self.cut, self.ring_at
        if k == at.nz - 1:
            return
        self.ring_at += 1
        last = self.ring_at == at.nz - 1

        def step(total, kept):
            total = total.astype(f32) + pick(kept, (at.z - 2 - k + at.nz) % at.nz).astype(f32)
            if not last:
                return total.astype(bf16)
            if self.pairs:
                low, high = total[..., :cut], total[..., cut:]
                return (
                    jnp.concatenate([pick(low, at.x), pick(high, at.y)], axis=-1),
                    pick(low, 1 - at.x).astype(bf16),
                    pick(high, 1 - at.y).astype(bf16),
                )
            return total

        came = self.line.done(self.total)
        total = self.line.run(step, came, self.kept)
        if not last:
            self.total = self.line.start(total, at.to_z)
        elif self.pairs:
            self.total, self.low, self.high = total
        else:
            self.total = total

    def last_step(self):
        for _ in range(self.at.nz):
            self.ring()

    def last_start(self):
        self.last_step()
        self.low = self.line.start(self.low, self.at.to_x)
        self.high = self.line.start(self.high, self.at.to_y)

    def last(self):
        rows = self.at.own_rows
        self.last_step()

        def step(total, *came):
            if came:
                total = total + jnp.concatenate(came, axis=-1).astype(f32)
            low, high = total[:rows], total[rows:]
            return jnp.where(self.at.c == 0, low, high), jnp.where(self.at.c == 0, high, low)

        came = self.line.done(self.low, self.high) if self.pairs else ()
        self.mine, theirs = self.line.run(step, self.total, *came)
        self.theirs = self.line.start(theirs, self.at.to_core)

    def result(self):
        theirs = self.line.done(self.theirs)
        return (
            jnp.where(self.at.c == 0, self.mine, theirs),
            jnp.where(self.at.c == 0, theirs, self.mine),
        )


class Sums:
    def __init__(self, line, at, value):
        self.line, self.value = line, value
        self.steps = [at.to_core, at.to_x, at.to_y] + at.z_swaps
        self.going = None

    def step(self):
        if self.going is not None:
            came = self.line.done(self.going)
            self.value = self.line.run(lambda v, c: v + c, self.value, came)
        self.going = self.line.start(self.value, self.steps.pop(0)) if self.steps else None

    def result(self):
        while self.going is not None:
            self.step()
        return self.value


CHUNK = 512
CHUNK_FORWARD = 1024


def window(h, wide):
    start = pl.multiple_of(jnp.minimum((h * HD) // LANE, (wide - WIN) // LANE) * LANE, LANE)
    return start, h * HD - start


def lane_masks(off, rows):
    lane = lax.broadcasted_iota(jnp.int32, (rows, WIN), 1)
    return (lane >= off) & (lane < off + HD), lane >= WIN - 4


def attend_kernel(first, last, wide, qkv_ref, qf_ref, kf_ref, old_ref, old_lse, out_ref, lse_ref):
    n = qkv_ref.shape[0]
    scale = (HD ** -0.5) * 1.4426950408889634
    zero = jnp.zeros((), bf16)
    if first == 0:
        out_ref[...] = jnp.zeros_like(out_ref)
    else:
        lse_ref[...] = old_lse[...]
        out_ref[...] = old_ref[...]

    def head(h, carry):
        start, off = window(h, wide)
        inside, feature = lane_masks(off, n)
        at = pl.ds(start, WIN)
        k = qkv_ref[:, pl.ds(start + wide, WIN)]
        k = jnp.where(inside, k, jnp.where(feature, kf_ref[...], zero))
        v_t = jnp.where(inside, qkv_ref[:, pl.ds(start + 2 * wide, WIN)], zero).T
        for i in range(n // CHUNK_FORWARD):
            rows = slice(i * CHUNK_FORWARD, (i + 1) * CHUNK_FORWARD)
            q = jnp.where(feature[:CHUNK_FORWARD], qf_ref[rows, :], qkv_ref[rows, at])
            s = lax.dot_general(k, q, NT, preferred_element_type=f32)
            top = jnp.max(s, axis=0, keepdims=True) * scale
            p = jnp.exp2(s * scale - top)
            total = jnp.sum(p, axis=0, keepdims=True)
            o_t = lax.dot_general(v_t, p.astype(bf16), NN, preferred_element_type=f32)
            out = (o_t / total).T.astype(bf16)
            out_ref[rows, at] = jnp.where(inside[:CHUNK_FORWARD], out, out_ref[rows, at])
            lse_ref[pl.ds(h, 1), rows] = top + jnp.log2(total)
        return carry

    lax.fori_loop(first, last, head, 0)


def attend(first, last, qkv, qf, kf, *old):
    n, wide = qkv.shape[0], qkv.shape[1] // 3
    heads = H // 2
    if not old:
        old = (jnp.zeros((16, LANE), bf16), jnp.zeros((8, LANE), f32))
    return tuple(
        pl.pallas_call(
            functools.partial(attend_kernel, first, last, wide),
            out_shape=(
                jax.ShapeDtypeStruct((n, wide), bf16),
                jax.ShapeDtypeStruct((heads, n), f32),
            ),
            compiler_params=pltpu.CompilerParams(vmem_limit_bytes=28 * 1024 * 1024),
            cost_estimate=COST,
        )(qkv, qf, kf, *old)
    )


def back_kernel(first, last, wide, qkv_ref, do_ref, qf_ref, kf_ref, lse_ref, old_ref, out_ref):
    n = qkv_ref.shape[0]
    scale = HD ** -0.5
    scale_two = scale * 1.4426950408889634
    zero = jnp.zeros((), bf16)
    if first == 0:
        out_ref[...] = jnp.zeros_like(out_ref)
    else:
        out_ref[...] = old_ref[...]

    def head(h, carry):
        start, off = window(h, wide)
        inside, feature = lane_masks(off, n)
        at = pl.ds(start, WIN)
        at_k, at_v = pl.ds(start + wide, WIN), pl.ds(start + 2 * wide, WIN)
        k_win = qkv_ref[:, at_k]
        k = jnp.where(inside, k_win, jnp.where(feature, kf_ref[...], zero))
        k_t = jnp.where(inside, k_win, zero).T
        v = qkv_ref[:, at_v]
        dk, dv = None, None
        for i in range(n // CHUNK):
            rows = slice(i * CHUNK, (i + 1) * CHUNK)
            q_win = qkv_ref[rows, at]
            q = jnp.where(feature[:CHUNK], qf_ref[rows, :], q_win)
            q_only = jnp.where(inside[:CHUNK], q_win, zero)
            do = jnp.where(inside[:CHUNK], do_ref[rows, at], zero)
            s = lax.dot_general(k, q, NT, preferred_element_type=f32)
            p = jnp.exp2(s * scale_two - lse_ref[pl.ds(h, 1), rows])
            dp = lax.dot_general(v, do, NT, preferred_element_type=f32)
            part = lax.dot_general(p.astype(bf16), do, NN, preferred_element_type=f32)
            dv = part if dv is None else dv + part
            inner = jnp.sum(p * dp, axis=0, keepdims=True)
            ds = (p * (dp - inner)).astype(bf16)
            part = lax.dot_general(ds, q_only, NN, preferred_element_type=f32)
            dk = part if dk is None else dk + part
            dq = lax.dot_general(k_t, ds, NN, preferred_element_type=f32).T
            dq = (dq * scale).astype(bf16)
            out_ref[rows, at] = jnp.where(inside[:CHUNK], dq, out_ref[rows, at])
        out_ref[:, at_k] = jnp.where(inside, (dk * scale).astype(bf16), out_ref[:, at_k])
        out_ref[:, at_v] = jnp.where(inside, dv.astype(bf16), out_ref[:, at_v])
        return carry

    lax.fori_loop(first, last, head, 0)


def attend_back(first, last, qkv, do, qf, kf, lse, *old):
    n, wide = qkv.shape[0], qkv.shape[1] // 3
    if not old:
        old = (jnp.zeros((16, LANE), bf16),)
    return pl.pallas_call(
        functools.partial(back_kernel, first, last, wide),
        out_shape=jax.ShapeDtypeStruct(qkv.shape, bf16),
        compiler_params=pltpu.CompilerParams(vmem_limit_bytes=36 * 1024 * 1024),
        cost_estimate=COST,
    )(qkv, do, qf, kf, lse, *old)


def norm_parts(values):
    center = jnp.mean(values, axis=-1, keepdims=True)
    centered = values - center
    spread = jnp.mean(centered * centered, axis=-1, keepdims=True)
    inverse = lax.rsqrt(spread + norm_epsilon)
    return centered * inverse, inverse


def out_norm_kernel(
    core_ref, x_ref, a_ref, b_ref, w_ref, v_ref, bias_ref, gain_ref, shift_ref, res_ref, norm_ref
):
    cut = w_ref.shape[1]
    width = x_ref.shape[1]
    half = width // 2
    a, b = a_ref[:, :half], b_ref[:, :half]
    mine = dot(a, w_ref[:half, :]) + dot(b, w_ref[half:, :])
    theirs = dot(a, v_ref[half:, :]) + dot(b, v_ref[:half, :])
    first = core_ref[0] == 0

    @pl.when(first)
    def _():
        res_ref[:, :cut] = mine
        res_ref[:, cut:] = theirs[:, : width - cut]

    @pl.when(jnp.logical_not(first))
    def _():
        res_ref[:, :cut] = theirs
        res_ref[:, cut:] = mine[:, : width - cut]

    values = res_ref[...] + x_ref[...].astype(f32) + bias_ref[...]
    res_ref[...] = values
    unit, _ = norm_parts(values)
    norm_ref[...] = (unit * gain_ref[...] + shift_ref[...]).astype(bf16)


def out_norm(core, x, a, b, w, v, bias, gain, shift):
    t, width = x.shape
    tile = 128
    rows = lambda cols: pl.BlockSpec((tile, cols), lambda i: (i, 0))
    all_of = lambda v: pl.BlockSpec(v.shape, lambda i: (0, 0))
    return tuple(
        pl.pallas_call(
            out_norm_kernel,
            grid=(t // tile,),
            out_shape=[
                jax.ShapeDtypeStruct((t, width), f32),
                jax.ShapeDtypeStruct((t, width), bf16),
            ],
            in_specs=[
                pl.BlockSpec(memory_space=pltpu.SMEM),
                rows(width), rows(a.shape[1]), rows(b.shape[1]), all_of(w), all_of(v),
                all_of(bias), all_of(gain), all_of(shift),
            ],
            out_specs=[rows(width), rows(width)],
            compiler_params=pltpu.CompilerParams(vmem_limit_bytes=16 * 1024 * 1024),
            cost_estimate=COST,
        )(core, x, a, b, w, v, bias, gain, shift)
    )


def norm_back_kernel(t_ref, came_ref, pass_ref, values_ref, gain_ref, out_ref, low_ref, sum_ref):
    t = t_ref[...] + came_ref[...].astype(f32)
    unit, inverse = norm_parts(values_ref[...].astype(f32))
    scaled = t * gain_ref[...]
    along = jnp.mean(scaled * unit, axis=-1, keepdims=True)
    grad = (scaled - jnp.mean(scaled, axis=-1, keepdims=True) - unit * along) * inverse
    grad = pass_ref[...].astype(f32) + grad
    out_ref[...] = grad
    low = grad.astype(bf16)
    low_ref[...] = low

    @pl.when(pl.program_id(0) == 0)
    def _():
        sum_ref[...] = jnp.zeros_like(sum_ref)

    sum_ref[0:1, :] += jnp.sum(t * unit, axis=0, keepdims=True)
    sum_ref[1:2, :] += jnp.sum(t, axis=0, keepdims=True)
    sum_ref[2:3, :] += jnp.sum(low.astype(f32), axis=0, keepdims=True)


def norm_back(t, came, passed, values, gain):
    n, width = t.shape
    tile = 128
    rows = pl.BlockSpec((tile, width), lambda i: (i, 0))
    return tuple(
        pl.pallas_call(
            norm_back_kernel,
            grid=(n // tile,),
            out_shape=[
                jax.ShapeDtypeStruct((n, width), f32),
                jax.ShapeDtypeStruct((n, width), bf16),
                jax.ShapeDtypeStruct((8, width), f32),
            ],
            in_specs=[rows] * 4 + [pl.BlockSpec((1, width), lambda i: (0, 0))],
            out_specs=[rows, rows, pl.BlockSpec((8, width), lambda i: (0, 0))],
            compiler_params=pltpu.CompilerParams(vmem_limit_bytes=16 * 1024 * 1024),
            cost_estimate=COST,
        )(t, came, passed, values, gain)
    )


def column_sum(rows):
    return jnp.sum(rows.astype(f32), axis=0)


def gelu_and_slope(z):
    root = 0.7978845608028654
    cube = 0.044715 * root
    square = z * z
    h = 0.5 + 0.5 * jnp.tanh(z * (root + cube * square))
    value = z * h
    return value, h + 2.0 * value * (1.0 - h) * (root + 3.0 * cube * square)


def up_kernel(n_ref, w_ref, b_ref, value_ref, slope_ref):
    cols = w_ref.shape[1]
    step = 512
    for left in range(0, cols, step):
        part = slice(left, min(left + step, cols))
        value, slope = gelu_and_slope(dot(n_ref[...], w_ref[:, part]) + b_ref[:, part])
        value_ref[:, part] = value.astype(bf16)
        slope_ref[:, part] = slope.astype(bf16)


def hidden_kernel(g_ref, w_ref, s_ref, out_ref, sum_ref):
    cols = w_ref.shape[1]
    step = 512

    @pl.when(pl.program_id(0) == 0)
    def _():
        sum_ref[...] = jnp.zeros_like(sum_ref)

    for left in range(0, cols, step):
        part = slice(left, min(left + step, cols))
        out = (dot(g_ref[...], w_ref[:, part]) * s_ref[:, part].astype(f32)).astype(bf16)
        out_ref[:, part] = out
        sum_ref[0:1, part] += jnp.sum(out.astype(f32), axis=0, keepdims=True)


def hidden_back(g, w, s):
    t, width = g.shape
    cols = w.shape[1]
    tile = 256
    row = pl.BlockSpec((tile, cols), lambda i: (i, 0))
    return tuple(
        pl.pallas_call(
            hidden_kernel,
            grid=(t // tile,),
            out_shape=[
                jax.ShapeDtypeStruct((t, cols), bf16),
                jax.ShapeDtypeStruct((8, cols), f32),
            ],
            in_specs=[
                pl.BlockSpec((tile, width), lambda i: (i, 0)),
                pl.BlockSpec(w.shape, lambda i: (0, 0)),
                row,
            ],
            out_specs=[row, pl.BlockSpec((8, cols), lambda i: (0, 0))],
            compiler_params=pltpu.CompilerParams(vmem_limit_bytes=28 * 1024 * 1024),
            cost_estimate=COST,
        )(g, w, s)
    )


def up_gelu(n, w, b):
    t, width = n.shape
    cols = w.shape[1]
    tile = 256
    out = pl.BlockSpec((tile, cols), lambda i: (i, 0))
    return tuple(
        pl.pallas_call(
            up_kernel,
            grid=(t // tile,),
            out_shape=[jax.ShapeDtypeStruct((t, cols), bf16)] * 2,
            in_specs=[
                pl.BlockSpec((tile, width), lambda i: (i, 0)),
                pl.BlockSpec(w.shape, lambda i: (0, 0)),
                pl.BlockSpec(b.shape, lambda i: (0, 0)),
            ],
            out_specs=[out, out],
            compiler_params=pltpu.CompilerParams(vmem_limit_bytes=28 * 1024 * 1024),
            cost_estimate=COST,
        )(n, w, b)
    )


def on_device(
    tokens,
    lengths,
    norm1_gain,
    norm1_bias,
    w_query,
    query_bias,
    w_key,
    w_value,
    value_bias,
    w_out,
    out_bias,
    norm2_gain,
    norm2_bias,
    w_up,
    up_bias,
    w_down,
    down_bias,
    cotangent,
):
    at = Places(lax.axis_size("rows"), lax.axis_size("seq"))
    line = Line()
    micro, rows_here, local_len, width = tokens.shape
    full_len = local_len * lax.axis_size("seq")
    own = 2 * rows_here * local_len
    own_rows, hidden_width = w_up.shape
    at.own_rows = own_rows
    chip_rows = 2 * own_rows
    zero_core = at.c == 0
    nz = at.nz
    head_width = width // 2
    wide = -(-head_width // LANE) * LANE
    out_cut = wide
    half_width = -(-hidden_width // (2 * LANE)) * LANE

    def by_core(a, b):
        return jnp.where(zero_core, a, b)

    def swapped_in(mine, came):
        low = jnp.where(at.x == 0, mine, came)
        high = jnp.where(at.x == 0, came, mine)
        return jnp.stack([low, high]).reshape(own, width)

    def for_swap_out(values):
        values = values.reshape(2, rows_here, local_len, width)
        return pick(values, at.x), pick(values, 1 - at.x).astype(bf16)

    def swapped_out(mine, came):
        came = came.astype(mine.dtype)
        return jnp.stack([jnp.where(at.x == 0, mine, came), jnp.where(at.x == 0, came, mine)])

    def fill(v, to):
        return jnp.pad(v, ((0, 0), (0, to - v.shape[1])))

    vectors = jnp.stack(
        [norm1_gain, norm1_bias, query_bias, value_bias, out_bias, norm2_gain, norm2_bias, down_bias]
    )
    vectors = dot(jnp.eye(own_rows, dtype=bf16), vectors, NT, bf16)
    me = lax.axis_index("rows") * lax.axis_size("seq") + lax.axis_index("seq")

    spot = jnp.arange(chip_rows, dtype=jnp.int32)
    spot = flip(at.c, spot // own_rows) * own_rows + spot % own_rows
    turn = (jnp.arange(chip_rows, dtype=jnp.int32)[:, None] == spot[None, :]).astype(bf16)
    u_cut, d_cut = 13 * LANE, 10 * LANE
    s_wide, u_wide, d_wide = 3 * wide, out_cut + half_width, half_width
    s_pieces = Pieces(at, chip_rows, s_wide)
    u_pieces = Pieces(at, chip_rows, u_wide)
    d_pieces = Pieces(at, chip_rows, d_wide)

    def qkv_half(c):
        part = slice(c * head_width, (c + 1) * head_width)
        query = fill(jnp.concatenate([w_query[:, part], vectors], axis=1), wide)
        return jnp.concatenate([query] + [fill(w[:, part], wide) for w in (w_key, w_value)], axis=1)

    def chip_shard(turn, keep, came):
        return dot(turn, jnp.concatenate([keep, came], axis=0), NN, bf16)

    def pair_parts(cut):
        def step(mine, low, high):
            pair = jnp.stack([mine, jnp.concatenate([low, high], axis=1)])
            return pair, pair[:, :, :cut], pair[:, :, cut:]

        return step

    def stack_parts(cut):
        def step(*v):
            return jnp.stack([p[..., :cut] for p in v]), jnp.stack([p[..., cut:] for p in v])

        return step

    def add_pair(pieces, k, array, cut):
        cols = pieces.cols
        pieces.add(
            array,
            [((a,), 0, (k, a, 0), 0, cut) for a in range(2)]
            + [((a,), cut, (k, 0, a), cut, cols - cut) for a in range(2)],
        )

    def indices(ks, array):
        return [((a,) if array.ndim == 3 else (i, a), k, a) for i, k in enumerate(ks) for a in (0, 1)]

    def add_low(pieces, ks, low, cut):
        pieces.add(low, [(i, 0, (k, a, 1), 0, cut) for i, k, a in indices(ks, low)])

    def add_high(pieces, ks, high, cut):
        wide = pieces.cols - cut
        pieces.add(high, [(i, 0, (k, 1, a), cut, wide) for i, k, a in indices(ks, high)])

    def add_across(pieces, ks, low, high, cut):
        add_low(pieces, ks, low, cut)
        add_high(pieces, ks, high, cut)

    def add_line(pieces, k, array, dx, dy):
        pieces.add(array, [((), 0, (k, dx, dy), 0, pieces.cols)])

    low, high = qkv_half(0), qkv_half(1)
    keep_s, give_s = by_core(low, high), by_core(high, low)
    core = line.start(give_s, at.to_core)
    up_full = fill(w_up, 2 * half_width)
    down_full = fill(dot(jnp.eye(own_rows, dtype=bf16), w_down, NT, bf16), 2 * half_width)
    low = [w_out[:, :out_cut], up_full[:, :half_width], down_full[:, :half_width]]
    high = [fill(w_out[:, out_cut:], out_cut), up_full[:, half_width:], down_full[:, half_width:]]
    low, high = jnp.concatenate(low, axis=1), jnp.concatenate(high, axis=1)
    keep_f, give_f = by_core(low, high), by_core(high, low)

    def other_shards(turn, keep, came):
        both = jnp.concatenate([keep, came], axis=0)
        u, d = dot(turn, both[:, :u_wide], NN, bf16), dot(turn, both[:, u_wide:], NN, bf16)
        return u, u[:, :u_cut], u[:, u_cut:], d, d[:, :d_cut], d[:, d_cut:]

    def tokens_step(tokens, came):
        return swapped_in(pick(tokens, at.x), came)

    def center_step(values):
        values = values.astype(f32)
        center = jnp.mean(values, axis=-1, keepdims=True)
        spread = jnp.mean((values - center) ** 2, axis=-1, keepdims=True)
        return center, lax.rsqrt(spread + norm_epsilon)

    ring = [line.run(chip_shard, turn, keep_s, line.done(core))]
    z, y = line.start(ring[0], at.to_z), line.start(ring[0], at.to_y)
    x = line.start(line.run(lambda v: pick(v, 1 - at.x), tokens), at.to_x)
    core = line.start(give_f, at.to_core)
    xs, ys = [], []
    ring.append(line.done(z))
    z = line.start(ring[-1], at.to_z)
    ys.append(line.done(y))
    y = line.start(ring[1], at.to_y)
    tokens_came = line.done(x)
    x = line.start(ring[0], at.to_x)
    core = line.done(core)
    shard_u, u_low, u_high, shard_d, d_low, d_high = line.run(other_shards, turn, keep_f, core)
    x_pair, y_pair = line.start(u_low, at.to_x), line.start(u_high, at.to_y)
    ring.append(line.done(z))
    z = line.start(ring[-1], at.to_z)
    ys.append(line.done(y))
    y = line.start(ring[2], at.to_y)
    xs.append(line.done(x))
    x = line.start(ring[1], at.to_x)
    u_low, u_high = line.done(x_pair, y_pair)
    u_pair, u_low, u_high = line.run(pair_parts(u_cut), shard_u, u_low, u_high)
    for k in range(3, nz):
        ring.append(line.done(z))
        if k < nz - 1:
            z = line.start(ring[-1], at.to_z)
    u_ring = [u_pair]
    z = line.start(u_pair, at.to_z)
    ys.append(line.done(y))
    y_more = [line.start(ring[k], at.to_y) for k in range(3, nz)]
    xs.append(line.done(x))
    x_more = [line.start(ring[k], at.to_x) for k in range(2, nz)]
    both = line.start(xs[0], at.to_y)
    tokens_own = line.run(tokens_step, tokens, tokens_came)
    u_ring.append(line.done(z))
    ys += [line.done(v) for v in y_more]
    xs += [line.done(v) for v in x_more]
    both = [line.done(both)]
    core = line.start(tokens_own, at.to_core)
    both_more = [line.start(xs[k], at.to_y) for k in range(1, nz)]
    z = line.start(u_ring[-1], at.to_z)
    tokens_all = line.run(lambda a, b: jnp.concatenate([a, b]), tokens_own, line.done(core))
    center, inverse_one = line.run(center_step, tokens_all)
    both += [line.done(v) for v in both_more]
    u_ring.append(line.done(z))
    x_pair, y_pair = line.start(d_low, at.to_x), line.start(d_high, at.to_y)
    x, y = line.start(u_high, at.to_x), line.start(u_low, at.to_y)
    z = line.start(u_ring[-1], at.to_z)

    row_lengths = pick(lengths, at.x)[0]
    ends_at = jnp.cumsum(row_lengths)
    inside = jnp.arange(own, dtype=jnp.int32)

    def segment_of(core):
        spots = (inside // local_len) * (full_len // 2) + core * local_len + inside % local_len
        return jnp.sum((spots[:, None] >= ends_at[None, :]).astype(jnp.int32), axis=-1)

    segments = jnp.concatenate([segment_of(at.c), segment_of(1 - at.c)])
    lane = (jnp.arange(WIN, dtype=jnp.int32) % 4)[None, :]
    feat_q = (segments[:, None] == lane).astype(bf16)
    feat_k = jnp.where(segments[:, None] == lane, 0.0, -BIG).astype(bf16)
    feat_q, feat_k = line.run(lambda *v: v, feat_q, feat_k)
    for k in range(nz):
        add_line(s_pieces, k, ring[k], 0, 0)
        add_line(s_pieces, k, xs[k], 1, 0)
        add_line(s_pieces, k, ys[k], 0, 1)
        add_line(s_pieces, k, both[k], 1, 1)

    weight_s = s_pieces.place(line, (s_wide,))
    chosen = jnp.eye(vectors.shape[1], s_wide, head_width, dtype=bf16)
    left = (head_width // LANE) * LANE
    vectors = line.run(
        lambda e, w: dot(e[:, left:wide], w[:, left:wide], NT), chosen, weight_s
    )
    gain_one, shift_one, bias_q, bias_v, bias_o, gain_two, shift_two, bias_d = [
        vectors[i][None] for i in range(8)
    ]
    halves = [by_core(b[:, :head_width], b[:, head_width:]) for b in (bias_q, bias_v)]
    bias_qkv = jnp.concatenate(
        [fill(halves[0], wide), jnp.zeros((1, wide), f32), fill(halves[1], wide)], axis=1
    )
    normed = line.run(
        lambda v, c, i, g, s: ((v.astype(f32) - c) * i * g + s).astype(bf16),
        tokens_all, center, inverse_one, gain_one, shift_one,
    )
    d_low, d_high, u_high, u_low = line.done(x_pair, y_pair, x, y)
    low, high = line.run(stack_parts(u_cut), u_ring[1])
    x, y = line.start(high, at.to_x), line.start(low, at.to_y)
    qkv = line.run(lambda n, w, b: (dot(n, w) + b).astype(bf16), normed, weight_s, bias_qkv)
    u_ring.append(line.done(z))
    high, low = line.done(x, y)
    for _ in range(4, nz):
        u_ring.append(line.done(line.start(u_ring[-1], at.to_z)))
    d_pair, d_low, d_high = line.run(pair_parts(d_cut), shard_d, d_low, d_high)
    add_pair(u_pieces, 0, u_pair, u_cut)
    add_across(u_pieces, [0], u_low, u_high, u_cut)
    add_across(u_pieces, [1], low, high, u_cut)
    parts = [line.run(stack_parts(u_cut), u) for u in u_ring[2:]]
    for k in range(1, nz):
        add_pair(u_pieces, k, u_ring[k], u_cut)
    heads = H // 2
    x, y = line.start(parts[0][1], at.to_x), line.start(parts[0][0], at.to_y)
    attended, lse = line.run(functools.partial(attend, 0, heads // 2), qkv, feat_q, feat_k)
    high, low = line.done(x, y)
    add_across(u_pieces, [2], low, high, u_cut)
    going = [
        (line.start(high, at.to_x), line.start(low, at.to_y)) for low, high in parts[1:]
    ]
    z = line.start(d_pair, at.to_z)
    attended, lse = line.run(
        functools.partial(attend, heads // 2, heads), qkv, feat_q, feat_k, attended, lse
    )
    for k, (x, y) in enumerate(going):
        high, low = line.done(x, y)
        add_across(u_pieces, [3 + k], low, high, u_cut)
    d_ring = [d_pair, line.done(z)]
    attended_own, give = line.run(
        lambda a: (a[:own], a[own:]), attended
    )
    core = line.start(give, at.to_core)
    z = line.start(d_ring[-1], at.to_z)
    cotangent_theirs = line.run(lambda v: pick(v, 1 - at.x), cotangent)
    x, y = line.start(cotangent_theirs, at.to_x), line.start(d_low, at.to_y)
    attended_other = line.done(core)
    weight_half_o, weight_u = u_pieces.place(line, (out_cut, half_width), (True, False))
    d_ring.append(line.done(z))
    out_came, d_low = line.done(x, y)
    core = line.start(weight_half_o, at.to_core)
    for _ in range(3, nz - 1):
        d_ring.append(line.done(line.start(d_ring[-1], at.to_z)))
    x = line.start(d_high, at.to_x)
    low, high = line.run(stack_parts(d_cut), *d_ring[1:])
    y = line.start(low, at.to_y)
    z = line.start(d_ring[-1], at.to_z)
    grad_out = line.run(
        lambda v, came: swapped_in(pick(v, at.x), came), cotangent, out_came
    )
    other_half_o = line.done(core)
    zero_flag = jnp.reshape(at.c, (1,)).astype(jnp.int32)
    residual_one, normed_two_own = line.run(
        out_norm, zero_flag, tokens_own, attended_own, attended_other, weight_half_o, other_half_o,
        bias_o, gain_two, shift_two,
    )
    add_pair(d_pieces, 0, d_pair, d_cut)
    d_high = line.done(x)
    add_across(d_pieces, [0], d_low, d_high, d_cut)
    low = line.done(y)
    d_ring.append(line.done(z))
    core = line.start(normed_two_own, at.to_core)
    x = line.start(high, at.to_x)
    low_last, high_last = line.run(stack_parts(d_cut), d_ring[-1])
    y, x_last = line.start(low_last, at.to_y), line.start(high_last, at.to_x)
    normed_two = line.run(
        lambda a, b: jnp.concatenate([a, b]), normed_two_own, line.done(core)
    )
    bias_up = fill(up_bias.astype(f32)[None], 2 * half_width)
    bias_up = by_core(bias_up[:, :half_width], bias_up[:, half_width:])

    def up_step(n, w, b):
        return up_gelu(n, w, b)

    active, slope = line.run(up_step, normed_two, weight_u, bias_up)
    high = line.done(x)
    add_across(d_pieces, list(range(1, nz - 1)), low, high, d_cut)
    low, high = line.done(y, x_last)
    add_across(d_pieces, [nz - 1], low, high, d_cut)
    for k in range(1, nz):
        add_pair(d_pieces, k, d_ring[k], d_cut)
    core = line.start(grad_out, at.to_core)
    weight_d = d_pieces.place(line, (half_width,))
    grad_out_all = line.run(lambda a, b: jnp.concatenate([a, b]), grad_out, line.done(core))

    d_down = line.run(lambda g, a: dot(g, a, TN, bf16), grad_out_all, active)
    quarter = nz // 4
    d_scatter = Scatter(line, at, d_cut, True, (quarter, 2 * quarter, 3 * quarter))
    d_scatter.cut_out(d_down)
    d_scatter.begin()
    grad_hidden, hidden_sums = line.run(hidden_back, grad_out_all, weight_d, slope)
    d_scatter.arrive()
    hidden_sums = hidden_sums[0]

    def rows_other(a, w):
        return dot(a[own:], w, NT, bf16)

    def rows_own(a, w):
        return dot(a[:own], w, NT)

    d_scatter.begin()
    give = line.run(rows_other, grad_hidden, weight_u)
    back_own = line.run(rows_own, grad_hidden, weight_u)
    d_scatter.arrive()
    core = line.start(give, at.to_core)
    d_scatter.begin()
    d_up = line.run(lambda n, g: dot(n, g, TN, bf16), normed_two, grad_hidden)
    core = line.done(core)
    d_scatter.arrive()
    d_scatter.begin()
    grad_residual, grad_branch, sums_two = line.run(
        norm_back, back_own, core, grad_out, residual_one, gain_two
    )

    def branch_columns(g):
        a, b = g[:, :out_cut], fill(g[:, out_cut:], out_cut)
        return by_core(a, b), by_core(b, a)

    branch_own, branch_peer = line.run(branch_columns, grad_branch)

    def heads_back(a, v, b, w):
        spare = ((0, wide - head_width), (0, 0))
        v, w = jnp.pad(v, spare), jnp.pad(w, spare)
        return (dot(a, v, NT) + dot(b, w, NT)).astype(bf16)

    def out_weight(a, b, g):
        return jnp.concatenate([dot(v, g, TN, bf16)[:head_width] for v in (a, b)])

    give = line.run(
        heads_back, branch_own, weight_half_o[head_width:], branch_peer, other_half_o[:head_width]
    )
    d_out_peer = line.run(out_weight, attended_other, attended_own, branch_peer)
    d_scatter.arrive()
    core = line.start(give, at.to_core)
    d_out_came = line.start(d_out_peer, at.to_core)
    d_scatter.keep()
    u_scatter = Scatter(line, at, u_cut, True, (nz // 2,))
    u_scatter.cut_out(d_up)
    u_scatter.begin()
    grad_att_own = line.run(
        heads_back, branch_own, weight_half_o[:head_width], branch_peer, other_half_o[head_width:]
    )
    grad_att = line.run(
        lambda a, b: jnp.concatenate([a, b]), grad_att_own, line.done(core)
    )

    def out_weight_own(a, b, g, came):
        total = jnp.concatenate([dot(v, g, TN)[:head_width] for v in (a, b)])
        total = total + came.astype(f32)
        half = total.shape[0] // 2
        low, high = total[:half], total[half:]
        return jnp.concatenate([by_core(low, high), by_core(high, low)]).astype(bf16)

    d_out = line.run(
        out_weight_own, attended_own, attended_other, branch_own, line.done(d_out_came)
    )
    d_scatter.arrive()
    u_scatter.arrive()
    d_scatter.ring()
    u_scatter.begin()
    u_scatter.more(d_out)
    d_qkv = line.run(
        functools.partial(attend_back, 0, heads // 2), qkv, grad_att, feat_q, feat_k, lse
    )
    d_scatter.arrive()
    u_scatter.arrive()
    d_scatter.ring()
    u_scatter.keep()
    d_qkv = line.run(
        functools.partial(attend_back, heads // 2, heads), qkv, grad_att, feat_q, feat_k, lse, d_qkv
    )
    d_scatter.arrive()
    d_scatter.last_start()
    s_scatter = Scatter(line, at, 8 * LANE, False)
    d_s = line.run(lambda n, g: dot(n, g, TN, bf16), normed, d_qkv)
    give = line.run(rows_other, d_qkv, weight_s)
    core = line.start(give, at.to_core)
    s_scatter.cut_out(d_s)
    s_scatter.begin()
    u_scatter.ring()
    back_own = line.run(rows_own, d_qkv, weight_s)
    d_scatter.last()
    grad_tokens, _, sums_one = line.run(
        norm_back, back_own, line.done(core), grad_residual, tokens_own, gain_one
    )
    token_mine, token_theirs = line.run(for_swap_out, grad_tokens)
    token_came = line.start(token_theirs, at.to_x)
    give = line.run(rows_other, active, weight_d)
    result_own = line.run(rows_own, active, weight_d)
    s_scatter.arrive()
    u_scatter.arrive()
    def full(half):
        zeros = jnp.zeros_like(half)
        return jnp.concatenate([by_core(half, zeros), by_core(zeros, half)])

    qkv_sums = column_sum(d_qkv)
    sums = jnp.concatenate(
        [
            column_sum(grad_out),
            sums_two[2],
            sums_two[0],
            sums_two[1],
            full(qkv_sums[:head_width]),
            full(qkv_sums[2 * wide : 2 * wide + head_width]),
            sums_one[0],
            sums_one[1],
            full(hidden_sums),
        ]
    )
    sums = jnp.pad(sums, (0, -sums.shape[0] % (8 * LANE))).reshape(-1, LANE)
    sums = line.run(lambda v: v, sums)
    core = line.start(give, at.to_core)
    sums_at = Sums(line, at, sums)
    sums_at.step()
    s_scatter.keep()
    u_scatter.ring()
    block_output = line.run(
        lambda r, t, c, b: (r + t + c.astype(f32) + b).astype(bf16),
        residual_one, result_own, line.done(core), bias_d,
    )
    out_mine, out_theirs = line.run(for_swap_out, block_output)
    sums_at.step()
    out_came = line.start(out_theirs, at.to_x)
    s_scatter.arrive()
    s_scatter.second()
    u_scatter.arrive()
    sums_at.step()
    u_scatter.last_start()
    s_scatter.ring()
    sums_at.step()
    u_scatter.last()
    s_scatter.ring()
    sums_at.step()
    s_scatter.last()
    sums_at.step()
    sums = sums_at.result()
    grad_tokens = swapped_out(token_mine, line.done(token_came))
    block_output = swapped_out(out_mine, line.done(out_came))
    sums = sums.reshape(-1)

    def my_part(i):
        return lax.dynamic_slice_in_dim(sums, i * width + me * own_rows, own_rows)

    def joined(parts, left, right):
        return jnp.concatenate([p[:, left:right] for p in parts], axis=1)

    d_down, d_up, d_qkv = d_scatter.result(), u_scatter.result(), s_scatter.result()
    return (
        block_output,
        grad_tokens,
        my_part(6),
        my_part(7),
        joined(d_qkv, 0, head_width),
        my_part(4),
        joined(d_qkv, wide, wide + head_width),
        joined(d_qkv, 2 * wide, 2 * wide + head_width),
        my_part(5),
        joined(d_up, half_width, u_wide)[:, :width],
        my_part(1),
        my_part(2),
        my_part(3),
        joined(d_up, 0, half_width)[:, :hidden_width],
        sums[8 * width : 8 * width + hidden_width],
        joined(d_down, 0, half_width)[:, :hidden_width].T,
        my_part(0),
    )


def solution(mesh):
    feature = P(AXES)
    matrix = P(AXES, None)
    row = P(None, "rows", "seq", None)
    return jax.shard_map(
        on_device,
        mesh=mesh,
        in_specs=(
            row,
            P(None, "rows", None),
            feature,
            feature,
            matrix,
            feature,
            matrix,
            matrix,
            feature,
            matrix,
            feature,
            feature,
            feature,
            matrix,
            P(),
            P(None, AXES),
            feature,
            row,
        ),
        out_specs=(
            row,
            row,
            feature,
            feature,
            matrix,
            feature,
            matrix,
            matrix,
            feature,
            matrix,
            feature,
            feature,
            feature,
            matrix,
            P(),
            P(None, AXES),
            feature,
        ),
        check_vma=False,
    )
```

```python
import functools

import jax
import jax.numpy as jnp
from jax import lax
from jax.experimental import pallas as pl
from jax.experimental.pallas import tpu as pltpu
from jax.sharding import PartitionSpec as P

H = 16
HD = 72
AXES = ("rows", "seq")
norm_epsilon = 1e-06
BIG = 1e30
LANE = 128
WIN = 256
bf16 = jnp.bfloat16
f32 = jnp.float32
COST = pl.CostEstimate(flops=5 * 10**9, bytes_accessed=10**7, transcendentals=10**6)
NT = (((1,), (1,)), ((), ()))
TN = (((0,), (0,)), ((), ()))
NN = (((1,), (0,)), ((), ()))


def dot(a, b, dims=NN, out=f32):
    return lax.dot_general(a, b, dims, preferred_element_type=f32).astype(out)


class Places:
    def __init__(self, n_rows, n_seq):
        self.nz, self.ny, self.nx, self.nc = n_rows // 2, 2, n_seq // 2, 2
        every = [
            (z, y, x, c)
            for z in range(self.nz)
            for y in range(2)
            for x in range(2)
            for c in range(2)
        ]
        nz = self.nz

        def flat(z, y, x, c):
            return ((z * 2 + y) * 2 + x) * 2 + c

        def pairs(f):
            return [(flat(*t), flat(*f(*t))) for t in every]

        self.to_core = pairs(lambda z, y, x, c: (z, y, x, 1 - c))
        self.to_x = pairs(lambda z, y, x, c: (z, y, 1 - x, c))
        self.to_y = pairs(lambda z, y, x, c: (z, 1 - y, x, c))
        self.to_z = pairs(lambda z, y, x, c: ((z + 1) % nz, y, x, c))
        assert nz & (nz - 1) == 0
        self.z_swaps = [
            pairs(lambda z, y, x, c, bit=1 << i: (z ^ bit, y, x, c))
            for i in range(nz.bit_length() - 1)
        ]
        r, s = lax.axis_index("rows"), lax.axis_index("seq")
        self.z, self.y, self.x, self.c = r // 2, r % 2, s // 2, s % 2


def send(value, pairs):
    return lax.ppermute(value, AXES, pairs)


class Going:
    def __init__(self, value):
        self.value, self.here = value, False


class Line:
    def __init__(self):
        self.token = jnp.zeros((8, LANE), f32)
        self.queue = []

    def pin(self, *values):
        return lax.optimization_barrier((values, self.token))[0]

    def close(self, *values):
        values, self.token = lax.optimization_barrier((values, self.token))
        return values if len(values) > 1 else values[0]

    def done(self, *going):
        while not all(g.here for g in going):
            first = self.queue.pop(0)
            first.value, first.here = self.close(first.value), True
        return [g.value for g in going] if len(going) > 1 else going[0].value

    def run(self, step, *values):
        out = step(*self.pin(*values))
        return self.close(*out) if isinstance(out, tuple) else self.close(out)

    def start(self, value, pairs):
        self.queue.append(Going(send(self.pin(value)[0], pairs)))
        return self.queue[-1]


def flip(here, by):
    return here + by - 2 * by * here


def place_kernel(n_in, n_out, plan, *refs):
    dyn = refs[0]
    ins, outs, sem = refs[1 : 1 + n_in], refs[1 + n_in : 1 + n_in + n_out], refs[1 + n_in + n_out]
    nz = outs[0].shape[0]
    copies = []
    for j, (i, src, src_col, out, dst, dst_col, wide) in enumerate(plan):
        zi, yi, xi = dst(dyn[0], dyn[1], dyn[2])
        zi = lax.rem(zi + dyn[3 + out], nz)
        source = ins[i].at[(*src, slice(None), pl.ds(src_col, wide))]
        target = outs[out].at[zi, yi, xi, :, pl.ds(dst_col, wide)]
        copies.append(pltpu.make_async_copy(source, target, sem.at[j]))
    for copy in copies:
        copy.start()
    for copy in copies:
        copy.wait()


def place(at, ins, plan, rows, widths, turned):
    turns = [jnp.where(at.c == 1, at.nz // 2 if t else 0, 0) for t in turned]
    cut_plan = []
    for i, src, src_col, dst, col, wide in plan:
        left = 0
        for out, out_wide in enumerate(widths):
            low, high = max(col, left), min(col + wide, left + out_wide)
            if low < high:
                cut_plan.append((i, src, src_col + low - col, out, dst, low - left, high - low))
            left += out_wide
    shapes = [(at.nz, 2, 2, rows, w) for w in widths]
    if rows % 8 == 0:
        dyn = jnp.stack([at.z, at.y, at.x, *turns]).astype(jnp.int32)
        outs = pl.pallas_call(
            functools.partial(place_kernel, len(ins), len(widths), cut_plan),
            out_shape=[jax.ShapeDtypeStruct(shape, ins[0].dtype) for shape in shapes],
            in_specs=[pl.BlockSpec(memory_space=pltpu.SMEM)]
            + [pl.BlockSpec(memory_space=pl.ANY)] * len(ins),
            out_specs=[pl.BlockSpec(memory_space=pltpu.VMEM)] * len(widths),
            scratch_shapes=[pltpu.SemaphoreType.DMA((len(cut_plan),))],
            compiler_params=pltpu.CompilerParams(vmem_limit_bytes=16 * 1024 * 1024),
            cost_estimate=COST,
        )(dyn, *ins)
    else:
        outs = [jnp.zeros(shape, ins[0].dtype) for shape in shapes]
        for i, src, src_col, out, dst, dst_col, wide in cut_plan:
            piece = ins[i][src][:, src_col : src_col + wide]
            zi, yi, xi = dst(at.z, at.y, at.x)
            zi = (zi + turns[out]) % at.nz
            outs[out] = lax.dynamic_update_slice(
                outs[out], piece[None, None, None], (zi, yi, xi, 0, dst_col)
            )
    return tuple(o.reshape(at.nz * 4 * rows, w) for o, w in zip(outs, widths))


class Pieces:
    def __init__(self, at, rows, cols):
        self.at, self.rows, self.cols = at, rows, cols
        self.arrays, self.plan = [], []

    def add(self, array, places):
        i, nz = len(self.arrays), self.at.nz
        self.arrays.append(array)
        for index, src_col, (k, dx, dy), col, wide in places:

            def slot(z, y, x, k=k, dx=dx, dy=dy):
                return lax.rem(z - k + nz, nz), flip(y, dy), flip(x, dx)

            self.plan.append((i, index, src_col, slot, col, wide))

    def place(self, line, widths, turned=(False, False)):
        return line.run(
            lambda *v: place(self.at, v, self.plan, self.rows, widths, turned[: len(widths)]),
            *self.arrays,
        )


def pick(values, i, axis=0):
    return lax.dynamic_index_in_dim(values, i, axis, keepdims=False)


class Scatter:
    def __init__(self, line, at, cut, pairs, ends=()):
        self.line, self.at, self.cut, self.pairs = line, at, cut, pairs
        self.ends = ends
        self.ring_at = 0
        self.total = self.low = self.high = self.extra = self.extra_came = None

    def blocks(self, total):
        at = self.at
        return total.reshape(at.nz, 2, 2, 2 * at.own_rows, total.shape[1])

    def cut_out(self, total):
        at, cut = self.at, self.cut
        self.whole = total
        self.low, self.high = [], []

        def step(total):
            v = self.blocks(total)
            low, high = pick(v[..., :cut], 1 - at.y, 1), pick(v[..., cut:], 1 - at.x, 2)
            ends = [0, *self.ends, at.nz]
            return tuple(v[i:j] for v in (low, high) for i, j in zip(ends[:-1], ends[1:]))

        self.parts = list(self.line.run(step, total))

    def begin(self):
        n = len(self.ends) + 1
        i = len(self.low)
        self.low.append(self.line.start(self.parts[i], self.at.to_y))
        self.high.append(self.line.start(self.parts[n + i], self.at.to_x))

    def more(self, total):
        self.extra = total
        part = self.line.run(lambda v: pick(self.blocks(v), 1 - self.at.x, 2), total)
        self.extra_came = self.line.start(part, self.at.to_x)

    def first_of(self, kept):
        return kept, pick(kept, (self.at.z - 1 + self.at.nz) % self.at.nz)

    def arrive(self):
        for going in (self.total, self.low, self.high, self.extra_came):
            if isinstance(going, Going):
                self.line.done(going)
            elif isinstance(going, list):
                self.line.done(*going)

    def keep_run(self):
        at, cut = self.at, self.cut
        came = self.line.done(*self.low, *self.high)
        n = len(self.low)
        extra = () if self.extra is None else (self.extra, self.line.done(self.extra_came))

        def step(total, *came):
            low, high = jnp.concatenate(came[:n]), jnp.concatenate(came[n : 2 * n])
            v = self.blocks(total)
            low = pick(v, at.y, 1)[..., :cut].astype(f32) + low.astype(f32)
            high = pick(v, at.x, 2)[..., cut:].astype(f32) + high.astype(f32)
            parts = [low, high]
            if extra:
                mine, other = came[2 * n :]
                parts.append(pick(self.blocks(mine), at.x, 2).astype(f32) + other.astype(f32))
            parts = [p.astype(bf16) for p in parts]
            if self.pairs:
                return self.first_of(jnp.concatenate(parts, axis=-1))
            low, high = parts
            return (
                pick(low, at.x, 1), pick(high, at.y, 1),
                pick(low, 1 - at.x, 1), pick(high, 1 - at.y, 1),
            )

        self.kept = self.line.run(step, self.whole, *came, *extra)
        self.whole = self.extra = self.extra_came = self.low = self.high = None

    def keep_start(self):
        kept = self.kept
        if self.pairs:
            self.kept = kept[0]
            self.total = self.line.start(kept[1], self.at.to_z)
        else:
            self.kept = kept[:2]
            self.low = self.line.start(kept[2], self.at.to_x)
            self.high = self.line.start(kept[3], self.at.to_y)

    def keep(self):
        self.keep_run()
        self.keep_start()

    def second(self):
        low, high = self.line.done(self.low, self.high)

        def step(kept_low, kept_high, low, high):
            low = (kept_low.astype(f32) + low.astype(f32)).astype(bf16)
            high = (kept_high.astype(f32) + high.astype(f32)).astype(bf16)
            return self.first_of(jnp.concatenate([low, high], axis=-1))

        self.kept, first = self.line.run(step, *self.kept, low, high)
        self.total = self.line.start(first, self.at.to_z)

    def ring(self):
        at, cut, k = self.at, self.cut, self.ring_at
        if k == at.nz - 1:
            return
        self.ring_at += 1
        last = self.ring_at == at.nz - 1

        def step(total, kept):
            total = total.astype(f32) + pick(kept, (at.z - 2 - k + at.nz) % at.nz).astype(f32)
            if not last:
                return total.astype(bf16)
            if self.pairs:
                low, high = total[..., :cut], total[..., cut:]
                return (
                    jnp.concatenate([pick(low, at.x), pick(high, at.y)], axis=-1),
                    pick(low, 1 - at.x).astype(bf16),
                    pick(high, 1 - at.y).astype(bf16),
                )
            return total

        came = self.line.done(self.total)
        total = self.line.run(step, came, self.kept)
        if not last:
            self.total = self.line.start(total, at.to_z)
        elif self.pairs:
            self.total, self.low, self.high = total
        else:
            self.total = total

    def last_step(self):
        for _ in range(self.at.nz):
            self.ring()

    def last_start(self):
        self.last_step()
        self.low = self.line.start(self.low, self.at.to_x)
        self.high = self.line.start(self.high, self.at.to_y)

    def last(self):
        rows = self.at.own_rows
        self.last_step()

        def step(total, *came):
            if came:
                total = total + jnp.concatenate(came, axis=-1).astype(f32)
            low, high = total[:rows], total[rows:]
            return jnp.where(self.at.c == 0, low, high), jnp.where(self.at.c == 0, high, low)

        came = self.line.done(self.low, self.high) if self.pairs else ()
        self.mine, theirs = self.line.run(step, self.total, *came)
        self.theirs = self.line.start(theirs, self.at.to_core)

    def result(self):
        theirs = self.line.done(self.theirs)
        return (
            jnp.where(self.at.c == 0, self.mine, theirs),
            jnp.where(self.at.c == 0, theirs, self.mine),
        )


class Sums:
    def __init__(self, line, at, value):
        self.line, self.value = line, value
        self.steps = [at.to_core, at.to_x, at.to_y] + at.z_swaps
        self.going = None

    def step(self):
        if self.going is not None:
            came = self.line.done(self.going)
            self.value = self.line.run(lambda v, c: v + c, self.value, came)
        self.going = self.line.start(self.value, self.steps.pop(0)) if self.steps else None

    def result(self):
        while self.going is not None:
            self.step()
        return self.value


CHUNK = 512
CHUNK_FORWARD = 1024


def window(h, wide):
    start = pl.multiple_of(jnp.minimum((h * HD) // LANE, (wide - WIN) // LANE) * LANE, LANE)
    return start, h * HD - start


def lane_masks(off, rows):
    lane = lax.broadcasted_iota(jnp.int32, (rows, WIN), 1)
    return (lane >= off) & (lane < off + HD), lane >= WIN - 4


def attend_kernel(first, last, wide, qkv_ref, qf_ref, kf_ref, old_ref, old_lse, out_ref, lse_ref):
    n = qkv_ref.shape[0]
    scale = (HD ** -0.5) * 1.4426950408889634
    zero = jnp.zeros((), bf16)
    if first == 0:
        out_ref[...] = jnp.zeros_like(out_ref)
    else:
        lse_ref[...] = old_lse[...]
        out_ref[...] = old_ref[...]

    def head(h, carry):
        start, off = window(h, wide)
        inside, feature = lane_masks(off, n)
        at = pl.ds(start, WIN)
        k = qkv_ref[:, pl.ds(start + wide, WIN)]
        k = jnp.where(inside, k, jnp.where(feature, kf_ref[...], zero))
        v_t = jnp.where(inside, qkv_ref[:, pl.ds(start + 2 * wide, WIN)], zero).T
        for i in range(n // CHUNK_FORWARD):
            rows = slice(i * CHUNK_FORWARD, (i + 1) * CHUNK_FORWARD)
            q = jnp.where(feature[:CHUNK_FORWARD], qf_ref[rows, :], qkv_ref[rows, at])
            s = lax.dot_general(k, q, NT, preferred_element_type=f32)
            top = jnp.max(s, axis=0, keepdims=True) * scale
            p = jnp.exp2(s * scale - top)
            total = jnp.sum(p, axis=0, keepdims=True)
            o_t = lax.dot_general(v_t, p.astype(bf16), NN, preferred_element_type=f32)
            out = (o_t / total).T.astype(bf16)
            out_ref[rows, at] = jnp.where(inside[:CHUNK_FORWARD], out, out_ref[rows, at])
            lse_ref[pl.ds(h, 1), rows] = top + jnp.log2(total)
        return carry

    lax.fori_loop(first, last, head, 0)


def attend(first, last, qkv, qf, kf, *old):
    n, wide = qkv.shape[0], qkv.shape[1] // 3
    heads = H // 2
    if not old:
        old = (jnp.zeros((16, LANE), bf16), jnp.zeros((8, LANE), f32))
    return tuple(
        pl.pallas_call(
            functools.partial(attend_kernel, first, last, wide),
            out_shape=(
                jax.ShapeDtypeStruct((n, wide), bf16),
                jax.ShapeDtypeStruct((heads, n), f32),
            ),
            compiler_params=pltpu.CompilerParams(vmem_limit_bytes=20 * 1024 * 1024),
            cost_estimate=COST,
        )(qkv, qf, kf, *old)
    )


def back_kernel(first, last, wide, qkv_ref, do_ref, qf_ref, kf_ref, lse_ref, old_ref, out_ref):
    n = qkv_ref.shape[0]
    scale = HD ** -0.5
    scale_two = scale * 1.4426950408889634
    zero = jnp.zeros((), bf16)
    if first == 0:
        out_ref[...] = jnp.zeros_like(out_ref)
    else:
        out_ref[...] = old_ref[...]

    def head(h, carry):
        start, off = window(h, wide)
        inside, feature = lane_masks(off, n)
        at = pl.ds(start, WIN)
        at_k, at_v = pl.ds(start + wide, WIN), pl.ds(start + 2 * wide, WIN)
        k_win = qkv_ref[:, at_k]
        k = jnp.where(inside, k_win, jnp.where(feature, kf_ref[...], zero))
        k_t = jnp.where(inside, k_win, zero).T
        v = qkv_ref[:, at_v]
        dk, dv = None, None
        for i in range(n // CHUNK):
            rows = slice(i * CHUNK, (i + 1) * CHUNK)
            q_win = qkv_ref[rows, at]
            q = jnp.where(feature[:CHUNK], qf_ref[rows, :], q_win)
            q_only = jnp.where(inside[:CHUNK], q_win, zero)
            do = jnp.where(inside[:CHUNK], do_ref[rows, at], zero)
            s = lax.dot_general(k, q, NT, preferred_element_type=f32)
            p = jnp.exp2(s * scale_two - lse_ref[pl.ds(h, 1), rows])
            dp = lax.dot_general(v, do, NT, preferred_element_type=f32)
            part = lax.dot_general(p.astype(bf16), do, NN, preferred_element_type=f32)
            dv = part if dv is None else dv + part
            inner = jnp.sum(p * dp, axis=0, keepdims=True)
            ds = (p * (dp - inner)).astype(bf16)
            part = lax.dot_general(ds, q_only, NN, preferred_element_type=f32)
            dk = part if dk is None else dk + part
            dq = lax.dot_general(k_t, ds, NN, preferred_element_type=f32).T
            dq = (dq * scale).astype(bf16)
            out_ref[rows, at] = jnp.where(inside[:CHUNK], dq, out_ref[rows, at])
        out_ref[:, at_k] = jnp.where(inside, (dk * scale).astype(bf16), out_ref[:, at_k])
        out_ref[:, at_v] = jnp.where(inside, dv.astype(bf16), out_ref[:, at_v])
        return carry

    lax.fori_loop(first, last, head, 0)


def attend_back(first, last, qkv, do, qf, kf, lse, *old):
    n, wide = qkv.shape[0], qkv.shape[1] // 3
    if not old:
        old = (jnp.zeros((16, LANE), bf16),)
    return pl.pallas_call(
        functools.partial(back_kernel, first, last, wide),
        out_shape=jax.ShapeDtypeStruct(qkv.shape, bf16),
        compiler_params=pltpu.CompilerParams(vmem_limit_bytes=26 * 1024 * 1024),
        cost_estimate=COST,
    )(qkv, do, qf, kf, lse, *old)


def norm_parts(values):
    center = jnp.mean(values, axis=-1, keepdims=True)
    centered = values - center
    spread = jnp.mean(centered * centered, axis=-1, keepdims=True)
    inverse = lax.rsqrt(spread + norm_epsilon)
    return centered * inverse, inverse


def out_norm_kernel(
    core_ref, x_ref, a_ref, b_ref, w_ref, v_ref, bias_ref, gain_ref, shift_ref, res_ref, norm_ref
):
    cut = w_ref.shape[1]
    width = x_ref.shape[1]
    half = width // 2
    a, b = a_ref[:, :half], b_ref[:, :half]
    mine = dot(a, w_ref[:half, :]) + dot(b, w_ref[half:, :])
    theirs = dot(a, v_ref[half:, :]) + dot(b, v_ref[:half, :])
    first = core_ref[0] == 0

    @pl.when(first)
    def _():
        res_ref[:, :cut] = mine
        res_ref[:, cut:] = theirs[:, : width - cut]

    @pl.when(jnp.logical_not(first))
    def _():
        res_ref[:, :cut] = theirs
        res_ref[:, cut:] = mine[:, : width - cut]

    values = res_ref[...] + x_ref[...].astype(f32) + bias_ref[...]
    res_ref[...] = values
    unit, _ = norm_parts(values)
    norm_ref[...] = (unit * gain_ref[...] + shift_ref[...]).astype(bf16)


def out_norm(core, x, a, b, w, v, bias, gain, shift):
    t, width = x.shape
    tile = 128
    rows = lambda cols: pl.BlockSpec((tile, cols), lambda i: (i, 0))
    all_of = lambda v: pl.BlockSpec(v.shape, lambda i: (0, 0))
    return tuple(
        pl.pallas_call(
            out_norm_kernel,
            grid=(t // tile,),
            out_shape=[
                jax.ShapeDtypeStruct((t, width), f32),
                jax.ShapeDtypeStruct((t, width), bf16),
            ],
            in_specs=[
                pl.BlockSpec(memory_space=pltpu.SMEM),
                rows(width), rows(a.shape[1]), rows(b.shape[1]), all_of(w), all_of(v),
                all_of(bias), all_of(gain), all_of(shift),
            ],
            out_specs=[rows(width), rows(width)],
            compiler_params=pltpu.CompilerParams(vmem_limit_bytes=16 * 1024 * 1024),
            cost_estimate=COST,
        )(core, x, a, b, w, v, bias, gain, shift)
    )


def norm_back_kernel(t_ref, came_ref, pass_ref, values_ref, gain_ref, out_ref, low_ref, sum_ref):
    t = t_ref[...] + came_ref[...].astype(f32)
    unit, inverse = norm_parts(values_ref[...].astype(f32))
    scaled = t * gain_ref[...]
    along = jnp.mean(scaled * unit, axis=-1, keepdims=True)
    grad = (scaled - jnp.mean(scaled, axis=-1, keepdims=True) - unit * along) * inverse
    grad = pass_ref[...].astype(f32) + grad
    out_ref[...] = grad
    low = grad.astype(bf16)
    low_ref[...] = low

    @pl.when(pl.program_id(0) == 0)
    def _():
        sum_ref[...] = jnp.zeros_like(sum_ref)

    sum_ref[0:1, :] += jnp.sum(t * unit, axis=0, keepdims=True)
    sum_ref[1:2, :] += jnp.sum(t, axis=0, keepdims=True)
    sum_ref[2:3, :] += jnp.sum(low.astype(f32), axis=0, keepdims=True)


def norm_back(t, came, passed, values, gain):
    n, width = t.shape
    tile = 128
    rows = pl.BlockSpec((tile, width), lambda i: (i, 0))
    return tuple(
        pl.pallas_call(
            norm_back_kernel,
            grid=(n // tile,),
            out_shape=[
                jax.ShapeDtypeStruct((n, width), f32),
                jax.ShapeDtypeStruct((n, width), bf16),
                jax.ShapeDtypeStruct((8, width), f32),
            ],
            in_specs=[rows] * 4 + [pl.BlockSpec((1, width), lambda i: (0, 0))],
            out_specs=[rows, rows, pl.BlockSpec((8, width), lambda i: (0, 0))],
            compiler_params=pltpu.CompilerParams(vmem_limit_bytes=16 * 1024 * 1024),
            cost_estimate=COST,
        )(t, came, passed, values, gain)
    )


def column_sum(rows):
    return jnp.sum(rows.astype(f32), axis=0)


def gelu_and_slope(z):
    root = 0.7978845608028654
    cube = 0.044715 * root
    square = z * z
    h = 0.5 + 0.5 * jnp.tanh(z * (root + cube * square))
    value = z * h
    return value, h + 2.0 * value * (1.0 - h) * (root + 3.0 * cube * square)


def up_kernel(n_ref, w_ref, b_ref, value_ref, slope_ref):
    cols = w_ref.shape[1]
    step = 512
    for left in range(0, cols, step):
        part = slice(left, min(left + step, cols))
        value, slope = gelu_and_slope(dot(n_ref[...], w_ref[:, part]) + b_ref[:, part])
        value_ref[:, part] = value.astype(bf16)
        slope_ref[:, part] = slope.astype(bf16)


def hidden_kernel(g_ref, w_ref, s_ref, out_ref, sum_ref):
    cols = w_ref.shape[1]
    step = 512

    @pl.when(pl.program_id(0) == 0)
    def _():
        sum_ref[...] = jnp.zeros_like(sum_ref)

    for left in range(0, cols, step):
        part = slice(left, min(left + step, cols))
        out = (dot(g_ref[...], w_ref[:, part]) * s_ref[:, part].astype(f32)).astype(bf16)
        out_ref[:, part] = out
        sum_ref[0:1, part] += jnp.sum(out.astype(f32), axis=0, keepdims=True)


def hidden_back(g, w, s):
    t, width = g.shape
    cols = w.shape[1]
    tile = 256
    row = pl.BlockSpec((tile, cols), lambda i: (i, 0))
    return tuple(
        pl.pallas_call(
            hidden_kernel,
            grid=(t // tile,),
            out_shape=[
                jax.ShapeDtypeStruct((t, cols), bf16),
                jax.ShapeDtypeStruct((8, cols), f32),
            ],
            in_specs=[
                pl.BlockSpec((tile, width), lambda i: (i, 0)),
                pl.BlockSpec(w.shape, lambda i: (0, 0)),
                row,
            ],
            out_specs=[row, pl.BlockSpec((8, cols), lambda i: (0, 0))],
            compiler_params=pltpu.CompilerParams(vmem_limit_bytes=20 * 1024 * 1024),
            cost_estimate=COST,
        )(g, w, s)
    )


def up_gelu(n, w, b):
    t, width = n.shape
    cols = w.shape[1]
    tile = 256
    out = pl.BlockSpec((tile, cols), lambda i: (i, 0))
    return tuple(
        pl.pallas_call(
            up_kernel,
            grid=(t // tile,),
            out_shape=[jax.ShapeDtypeStruct((t, cols), bf16)] * 2,
            in_specs=[
                pl.BlockSpec((tile, width), lambda i: (i, 0)),
                pl.BlockSpec(w.shape, lambda i: (0, 0)),
                pl.BlockSpec(b.shape, lambda i: (0, 0)),
            ],
            out_specs=[out, out],
            compiler_params=pltpu.CompilerParams(vmem_limit_bytes=20 * 1024 * 1024),
            cost_estimate=COST,
        )(n, w, b)
    )


def on_device(
    tokens,
    lengths,
    norm1_gain,
    norm1_bias,
    w_query,
    query_bias,
    w_key,
    w_value,
    value_bias,
    w_out,
    out_bias,
    norm2_gain,
    norm2_bias,
    w_up,
    up_bias,
    w_down,
    down_bias,
    cotangent,
):
    at = Places(lax.axis_size("rows"), lax.axis_size("seq"))
    line = Line()
    micro, rows_here, local_len, width = tokens.shape
    full_len = local_len * lax.axis_size("seq")
    own = 2 * rows_here * local_len
    own_rows, hidden_width = w_up.shape
    at.own_rows = own_rows
    chip_rows = 2 * own_rows
    zero_core = at.c == 0
    nz = at.nz
    head_width = width // 2
    wide = -(-head_width // LANE) * LANE
    out_cut = wide
    half_width = -(-hidden_width // (2 * LANE)) * LANE

    def by_core(a, b):
        return jnp.where(zero_core, a, b)

    def swapped_in(mine, came):
        low = jnp.where(at.x == 0, mine, came)
        high = jnp.where(at.x == 0, came, mine)
        return jnp.stack([low, high]).reshape(own, width)

    def for_swap_out(values):
        values = values.reshape(2, rows_here, local_len, width)
        return pick(values, at.x), pick(values, 1 - at.x).astype(bf16)

    def swapped_out(mine, came):
        came = came.astype(mine.dtype)
        return jnp.stack([jnp.where(at.x == 0, mine, came), jnp.where(at.x == 0, came, mine)])

    def fill(v, to):
        return jnp.pad(v, ((0, 0), (0, to - v.shape[1])))

    vectors = jnp.stack(
        [norm1_gain, norm1_bias, query_bias, value_bias, out_bias, norm2_gain, norm2_bias, down_bias]
    )
    vectors = dot(jnp.eye(own_rows, dtype=bf16), vectors, NT, bf16)
    me = lax.axis_index("rows") * lax.axis_size("seq") + lax.axis_index("seq")

    spot = jnp.arange(chip_rows, dtype=jnp.int32)
    spot = flip(at.c, spot // own_rows) * own_rows + spot % own_rows
    turn = (jnp.arange(chip_rows, dtype=jnp.int32)[:, None] == spot[None, :]).astype(bf16)
    u_cut, d_cut = 13 * LANE, 10 * LANE
    s_wide, u_wide, d_wide = 3 * wide, out_cut + half_width, half_width
    s_pieces = Pieces(at, chip_rows, s_wide)
    u_pieces = Pieces(at, chip_rows, u_wide)
    d_pieces = Pieces(at, chip_rows, d_wide)

    def qkv_half(c):
        part = slice(c * head_width, (c + 1) * head_width)
        query = fill(jnp.concatenate([w_query[:, part], vectors], axis=1), wide)
        return jnp.concatenate([query] + [fill(w[:, part], wide) for w in (w_key, w_value)], axis=1)

    def chip_shard(turn, keep, came):
        return dot(turn, jnp.concatenate([keep, came], axis=0), NN, bf16)

    def pair_parts(cut):
        def step(mine, low, high):
            pair = jnp.stack([mine, jnp.concatenate([low, high], axis=1)])
            return pair, pair[:, :, :cut], pair[:, :, cut:]

        return step

    def stack_parts(cut):
        def step(*v):
            return jnp.stack([p[..., :cut] for p in v]), jnp.stack([p[..., cut:] for p in v])

        return step

    def add_pair(pieces, k, array, cut):
        cols = pieces.cols
        pieces.add(
            array,
            [((a,), 0, (k, a, 0), 0, cut) for a in range(2)]
            + [((a,), cut, (k, 0, a), cut, cols - cut) for a in range(2)],
        )

    def indices(ks, array):
        return [((a,) if array.ndim == 3 else (i, a), k, a) for i, k in enumerate(ks) for a in (0, 1)]

    def add_low(pieces, ks, low, cut):
        pieces.add(low, [(i, 0, (k, a, 1), 0, cut) for i, k, a in indices(ks, low)])

    def add_high(pieces, ks, high, cut):
        wide = pieces.cols - cut
        pieces.add(high, [(i, 0, (k, 1, a), cut, wide) for i, k, a in indices(ks, high)])

    def add_across(pieces, ks, low, high, cut):
        add_low(pieces, ks, low, cut)
        add_high(pieces, ks, high, cut)

    def add_line(pieces, k, array, dx, dy):
        pieces.add(array, [((), 0, (k, dx, dy), 0, pieces.cols)])

    low, high = qkv_half(0), qkv_half(1)
    keep_s, give_s = by_core(low, high), by_core(high, low)
    core = line.start(give_s, at.to_core)
    up_full = fill(w_up, 2 * half_width)
    down_full = fill(dot(jnp.eye(own_rows, dtype=bf16), w_down, NT, bf16), 2 * half_width)
    low = [w_out[:, :out_cut], up_full[:, :half_width], down_full[:, :half_width]]
    high = [fill(w_out[:, out_cut:], out_cut), up_full[:, half_width:], down_full[:, half_width:]]
    low, high = jnp.concatenate(low, axis=1), jnp.concatenate(high, axis=1)
    keep_f, give_f = by_core(low, high), by_core(high, low)

    def other_shards(turn, keep, came):
        both = jnp.concatenate([keep, came], axis=0)
        u, d = dot(turn, both[:, :u_wide], NN, bf16), dot(turn, both[:, u_wide:], NN, bf16)
        return u, u[:, :u_cut], u[:, u_cut:], d, d[:, :d_cut], d[:, d_cut:]

    def tokens_step(tokens, came):
        return swapped_in(pick(tokens, at.x), came)

    def center_step(values):
        values = values.astype(f32)
        center = jnp.mean(values, axis=-1, keepdims=True)
        spread = jnp.mean((values - center) ** 2, axis=-1, keepdims=True)
        return center, lax.rsqrt(spread + norm_epsilon)

    ring = [line.run(chip_shard, turn, keep_s, line.done(core))]
    z, y = line.start(ring[0], at.to_z), line.start(ring[0], at.to_y)
    x = line.start(line.run(lambda v: pick(v, 1 - at.x), tokens), at.to_x)
    core = line.start(give_f, at.to_core)
    xs, ys = [], []
    ring.append(line.done(z))
    z = line.start(ring[-1], at.to_z)
    ys.append(line.done(y))
    y = line.start(ring[1], at.to_y)
    tokens_came = line.done(x)
    x = line.start(ring[0], at.to_x)
    core = line.done(core)
    shard_u, u_low, u_high, shard_d, d_low, d_high = line.run(other_shards, turn, keep_f, core)
    x_pair, y_pair = line.start(u_low, at.to_x), line.start(u_high, at.to_y)
    ring.append(line.done(z))
    z = line.start(ring[-1], at.to_z)
    ys.append(line.done(y))
    y = line.start(ring[2], at.to_y)
    xs.append(line.done(x))
    x = line.start(ring[1], at.to_x)
    u_low, u_high = line.done(x_pair, y_pair)
    u_pair, u_low, u_high = line.run(pair_parts(u_cut), shard_u, u_low, u_high)
    for k in range(3, nz):
        ring.append(line.done(z))
        if k < nz - 1:
            z = line.start(ring[-1], at.to_z)
    u_ring = [u_pair]
    z = line.start(u_pair, at.to_z)
    ys.append(line.done(y))
    y_more = [line.start(ring[k], at.to_y) for k in range(3, nz)]
    xs.append(line.done(x))
    x_more = [line.start(ring[k], at.to_x) for k in range(2, nz)]
    both = line.start(xs[0], at.to_y)
    tokens_own = line.run(tokens_step, tokens, tokens_came)
    u_ring.append(line.done(z))
    ys += [line.done(v) for v in y_more]
    xs += [line.done(v) for v in x_more]
    both = [line.done(both)]
    core = line.start(tokens_own, at.to_core)
    both_more = [line.start(xs[k], at.to_y) for k in range(1, nz)]
    z = line.start(u_ring[-1], at.to_z)
    tokens_all = line.run(lambda a, b: jnp.concatenate([a, b]), tokens_own, line.done(core))
    center, inverse_one = line.run(center_step, tokens_all)
    both += [line.done(v) for v in both_more]
    u_ring.append(line.done(z))
    x_pair, y_pair = line.start(d_low, at.to_x), line.start(d_high, at.to_y)
    x, y = line.start(u_high, at.to_x), line.start(u_low, at.to_y)
    z = line.start(u_ring[-1], at.to_z)

    row_lengths = pick(lengths, at.x)[0]
    ends_at = jnp.cumsum(row_lengths)
    inside = jnp.arange(own, dtype=jnp.int32)

    def segment_of(core):
        spots = (inside // local_len) * (full_len // 2) + core * local_len + inside % local_len
        return jnp.sum((spots[:, None] >= ends_at[None, :]).astype(jnp.int32), axis=-1)

    segments = jnp.concatenate([segment_of(at.c), segment_of(1 - at.c)])
    lane = (jnp.arange(WIN, dtype=jnp.int32) % 4)[None, :]
    feat_q = (segments[:, None] == lane).astype(bf16)
    feat_k = jnp.where(segments[:, None] == lane, 0.0, -BIG).astype(bf16)
    feat_q, feat_k = line.run(lambda *v: v, feat_q, feat_k)
    for k in range(nz):
        add_line(s_pieces, k, ring[k], 0, 0)
        add_line(s_pieces, k, xs[k], 1, 0)
        add_line(s_pieces, k, ys[k], 0, 1)
        add_line(s_pieces, k, both[k], 1, 1)

    weight_s = s_pieces.place(line, (s_wide,))
    chosen = jnp.eye(vectors.shape[1], s_wide, head_width, dtype=bf16)
    left = (head_width // LANE) * LANE
    vectors = line.run(
        lambda e, w: dot(e[:, left:wide], w[:, left:wide], NT), chosen, weight_s
    )
    gain_one, shift_one, bias_q, bias_v, bias_o, gain_two, shift_two, bias_d = [
        vectors[i][None] for i in range(8)
    ]
    halves = [by_core(b[:, :head_width], b[:, head_width:]) for b in (bias_q, bias_v)]
    bias_qkv = jnp.concatenate(
        [fill(halves[0], wide), jnp.zeros((1, wide), f32), fill(halves[1], wide)], axis=1
    )
    normed = line.run(
        lambda v, c, i, g, s: ((v.astype(f32) - c) * i * g + s).astype(bf16),
        tokens_all, center, inverse_one, gain_one, shift_one,
    )
    d_low, d_high, u_high, u_low = line.done(x_pair, y_pair, x, y)
    low, high = line.run(stack_parts(u_cut), u_ring[1])
    x, y = line.start(high, at.to_x), line.start(low, at.to_y)
    qkv = line.run(lambda n, w, b: (dot(n, w) + b).astype(bf16), normed, weight_s, bias_qkv)
    u_ring.append(line.done(z))
    high, low = line.done(x, y)
    for _ in range(4, nz):
        u_ring.append(line.done(line.start(u_ring[-1], at.to_z)))
    d_pair, d_low, d_high = line.run(pair_parts(d_cut), shard_d, d_low, d_high)
    add_pair(u_pieces, 0, u_pair, u_cut)
    add_across(u_pieces, [0], u_low, u_high, u_cut)
    add_across(u_pieces, [1], low, high, u_cut)
    parts = [line.run(stack_parts(u_cut), u) for u in u_ring[2:]]
    for k in range(1, nz):
        add_pair(u_pieces, k, u_ring[k], u_cut)
    heads = H // 2
    x, y = line.start(parts[0][1], at.to_x), line.start(parts[0][0], at.to_y)
    attended, lse = line.run(functools.partial(attend, 0, heads // 2), qkv, feat_q, feat_k)
    high, low = line.done(x, y)
    add_across(u_pieces, [2], low, high, u_cut)
    going = [
        (line.start(high, at.to_x), line.start(low, at.to_y)) for low, high in parts[1:]
    ]
    z = line.start(d_pair, at.to_z)
    attended, lse = line.run(
        functools.partial(attend, heads // 2, heads), qkv, feat_q, feat_k, attended, lse
    )
    for k, (x, y) in enumerate(going):
        high, low = line.done(x, y)
        add_across(u_pieces, [3 + k], low, high, u_cut)
    d_ring = [d_pair, line.done(z)]
    attended_own, give = line.run(
        lambda a: (a[:own], a[own:]), attended
    )
    core = line.start(give, at.to_core)
    z = line.start(d_ring[-1], at.to_z)
    cotangent_theirs = line.run(lambda v: pick(v, 1 - at.x), cotangent)
    x, y = line.start(cotangent_theirs, at.to_x), line.start(d_low, at.to_y)
    attended_other = line.done(core)
    weight_half_o, weight_u = u_pieces.place(line, (out_cut, half_width), (True, False))
    d_ring.append(line.done(z))
    out_came, d_low = line.done(x, y)
    core = line.start(weight_half_o, at.to_core)
    for _ in range(3, nz - 1):
        d_ring.append(line.done(line.start(d_ring[-1], at.to_z)))
    x = line.start(d_high, at.to_x)
    low, high = line.run(stack_parts(d_cut), *d_ring[1:])
    y = line.start(low, at.to_y)
    z = line.start(d_ring[-1], at.to_z)
    grad_out = line.run(
        lambda v, came: swapped_in(pick(v, at.x), came), cotangent, out_came
    )
    other_half_o = line.done(core)
    zero_flag = jnp.reshape(at.c, (1,)).astype(jnp.int32)
    residual_one, normed_two_own = line.run(
        out_norm, zero_flag, tokens_own, attended_own, attended_other, weight_half_o, other_half_o,
        bias_o, gain_two, shift_two,
    )
    add_pair(d_pieces, 0, d_pair, d_cut)
    d_high = line.done(x)
    add_across(d_pieces, [0], d_low, d_high, d_cut)
    low = line.done(y)
    d_ring.append(line.done(z))
    core = line.start(normed_two_own, at.to_core)
    x = line.start(high, at.to_x)
    low_last, high_last = line.run(stack_parts(d_cut), d_ring[-1])
    y, x_last = line.start(low_last, at.to_y), line.start(high_last, at.to_x)
    normed_two = line.run(
        lambda a, b: jnp.concatenate([a, b]), normed_two_own, line.done(core)
    )
    bias_up = fill(up_bias.astype(f32)[None], 2 * half_width)
    bias_up = by_core(bias_up[:, :half_width], bias_up[:, half_width:])

    def up_step(n, w, b):
        return up_gelu(n, w, b)

    active, slope = line.run(up_step, normed_two, weight_u, bias_up)
    high = line.done(x)
    add_across(d_pieces, list(range(1, nz - 1)), low, high, d_cut)
    low, high = line.done(y, x_last)
    add_across(d_pieces, [nz - 1], low, high, d_cut)
    for k in range(1, nz):
        add_pair(d_pieces, k, d_ring[k], d_cut)
    core = line.start(grad_out, at.to_core)
    weight_d = d_pieces.place(line, (half_width,))
    grad_out_all = line.run(lambda a, b: jnp.concatenate([a, b]), grad_out, line.done(core))

    d_down = line.run(lambda g, a: dot(g, a, TN, bf16), grad_out_all, active)
    quarter = nz // 4
    d_scatter = Scatter(line, at, d_cut, True, (quarter, 2 * quarter, 3 * quarter))
    d_scatter.cut_out(d_down)
    d_scatter.begin()
    grad_hidden, hidden_sums = line.run(hidden_back, grad_out_all, weight_d, slope)
    d_scatter.arrive()
    hidden_sums = hidden_sums[0]

    def rows_other(a, w):
        return dot(a[own:], w, NT, bf16)

    def rows_own(a, w):
        return dot(a[:own], w, NT)

    d_scatter.begin()
    give = line.run(rows_other, grad_hidden, weight_u)
    back_own = line.run(rows_own, grad_hidden, weight_u)
    d_scatter.arrive()
    core = line.start(give, at.to_core)
    d_scatter.begin()
    d_up = line.run(lambda n, g: dot(n, g, TN, bf16), normed_two, grad_hidden)
    core = line.done(core)
    d_scatter.arrive()
    d_scatter.begin()
    grad_residual, grad_branch, sums_two = line.run(
        norm_back, back_own, core, grad_out, residual_one, gain_two
    )

    def branch_columns(g):
        a, b = g[:, :out_cut], fill(g[:, out_cut:], out_cut)
        return by_core(a, b), by_core(b, a)

    branch_own, branch_peer = line.run(branch_columns, grad_branch)

    def heads_back(a, v, b, w):
        spare = ((0, wide - head_width), (0, 0))
        v, w = jnp.pad(v, spare), jnp.pad(w, spare)
        return (dot(a, v, NT) + dot(b, w, NT)).astype(bf16)

    def out_weight(a, b, g):
        return jnp.concatenate([dot(v, g, TN, bf16)[:head_width] for v in (a, b)])

    give = line.run(
        heads_back, branch_own, weight_half_o[head_width:], branch_peer, other_half_o[:head_width]
    )
    d_out_peer = line.run(out_weight, attended_other, attended_own, branch_peer)
    d_scatter.arrive()
    core = line.start(give, at.to_core)
    d_out_came = line.start(d_out_peer, at.to_core)
    d_scatter.keep()
    u_scatter = Scatter(line, at, u_cut, True, (nz // 2,))
    u_scatter.cut_out(d_up)
    u_scatter.begin()
    grad_att_own = line.run(
        heads_back, branch_own, weight_half_o[:head_width], branch_peer, other_half_o[head_width:]
    )
    grad_att = line.run(
        lambda a, b: jnp.concatenate([a, b]), grad_att_own, line.done(core)
    )

    def out_weight_own(a, b, g, came):
        total = jnp.concatenate([dot(v, g, TN)[:head_width] for v in (a, b)])
        total = total + came.astype(f32)
        half = total.shape[0] // 2
        low, high = total[:half], total[half:]
        return jnp.concatenate([by_core(low, high), by_core(high, low)]).astype(bf16)

    d_out = line.run(
        out_weight_own, attended_own, attended_other, branch_own, line.done(d_out_came)
    )
    d_scatter.arrive()
    u_scatter.arrive()
    d_scatter.ring()
    u_scatter.begin()
    u_scatter.more(d_out)
    d_qkv = line.run(
        functools.partial(attend_back, 0, heads // 2), qkv, grad_att, feat_q, feat_k, lse
    )
    d_scatter.arrive()
    u_scatter.arrive()
    d_scatter.ring()
    u_scatter.keep()
    d_qkv = line.run(
        functools.partial(attend_back, heads // 2, heads), qkv, grad_att, feat_q, feat_k, lse, d_qkv
    )
    d_scatter.arrive()
    d_scatter.last_start()
    s_scatter = Scatter(line, at, 8 * LANE, False)
    d_s = line.run(lambda n, g: dot(n, g, TN, bf16), normed, d_qkv)
    give = line.run(rows_other, d_qkv, weight_s)
    core = line.start(give, at.to_core)
    s_scatter.cut_out(d_s)
    s_scatter.begin()
    u_scatter.ring()
    back_own = line.run(rows_own, d_qkv, weight_s)
    d_scatter.last()
    grad_tokens, _, sums_one = line.run(
        norm_back, back_own, line.done(core), grad_residual, tokens_own, gain_one
    )
    token_mine, token_theirs = line.run(for_swap_out, grad_tokens)
    token_came = line.start(token_theirs, at.to_x)
    give = line.run(rows_other, active, weight_d)
    result_own = line.run(rows_own, active, weight_d)
    s_scatter.arrive()
    u_scatter.arrive()
    def full(half):
        zeros = jnp.zeros_like(half)
        return jnp.concatenate([by_core(half, zeros), by_core(zeros, half)])

    qkv_sums = column_sum(d_qkv)
    sums = jnp.concatenate(
        [
            column_sum(grad_out),
            sums_two[2],
            sums_two[0],
            sums_two[1],
            full(qkv_sums[:head_width]),
            full(qkv_sums[2 * wide : 2 * wide + head_width]),
            sums_one[0],
            sums_one[1],
            full(hidden_sums),
        ]
    )
    sums = jnp.pad(sums, (0, -sums.shape[0] % (8 * LANE))).reshape(-1, LANE)
    sums = line.run(lambda v: v, sums)
    core = line.start(give, at.to_core)
    sums_at = Sums(line, at, sums)
    sums_at.step()
    s_scatter.keep()
    u_scatter.ring()
    block_output = line.run(
        lambda r, t, c, b: (r + t + c.astype(f32) + b).astype(bf16),
        residual_one, result_own, line.done(core), bias_d,
    )
    out_mine, out_theirs = line.run(for_swap_out, block_output)
    sums_at.step()
    out_came = line.start(out_theirs, at.to_x)
    s_scatter.arrive()
    s_scatter.second()
    u_scatter.arrive()
    sums_at.step()
    u_scatter.last_start()
    s_scatter.ring()
    sums_at.step()
    u_scatter.last()
    s_scatter.ring()
    sums_at.step()
    s_scatter.last()
    sums_at.step()
    sums = sums_at.result()
    grad_tokens = swapped_out(token_mine, line.done(token_came))
    block_output = swapped_out(out_mine, line.done(out_came))
    sums = sums.reshape(-1)

    def my_part(i):
        return lax.dynamic_slice_in_dim(sums, i * width + me * own_rows, own_rows)

    def joined(parts, left, right):
        return jnp.concatenate([p[:, left:right] for p in parts], axis=1)

    d_down, d_up, d_qkv = d_scatter.result(), u_scatter.result(), s_scatter.result()
    return (
        block_output,
        grad_tokens,
        my_part(6),
        my_part(7),
        joined(d_qkv, 0, head_width),
        my_part(4),
        joined(d_qkv, wide, wide + head_width),
        joined(d_qkv, 2 * wide, 2 * wide + head_width),
        my_part(5),
        joined(d_up, half_width, u_wide)[:, :width],
        my_part(1),
        my_part(2),
        my_part(3),
        joined(d_up, 0, half_width)[:, :hidden_width],
        sums[8 * width : 8 * width + hidden_width],
        joined(d_down, 0, half_width)[:, :hidden_width].T,
        my_part(0),
    )


def solution(mesh):
    feature = P(AXES)
    matrix = P(AXES, None)
    row = P(None, "rows", "seq", None)
    return jax.shard_map(
        on_device,
        mesh=mesh,
        in_specs=(
            row,
            P(None, "rows", None),
            feature,
            feature,
            matrix,
            feature,
            matrix,
            matrix,
            feature,
            matrix,
            feature,
            feature,
            feature,
            matrix,
            P(),
            P(None, AXES),
            feature,
            row,
        ),
        out_specs=(
            row,
            row,
            feature,
            feature,
            matrix,
            feature,
            matrix,
            matrix,
            feature,
            matrix,
            feature,
            feature,
            feature,
            matrix,
            P(),
            P(None, AXES),
            feature,
        ),
        check_vma=False,
    )
```
